32 devices in a mesh: side: 2 (over y), dev: 16 (over z, x, core).
Axes of the slice: x: 2, y: 2, z: 4, core: 2. Of those that a mesh axis runs over, the one named last changes fastest.
Arguments:
- queries: bfloat16 [512, 8192], P('dev', 'side'), may hold values from -6 to 6
- cache_keys: bfloat16 [512, 256, 512], P('dev', None, 'side'), may hold values from -6 to 6
- cache_values: bfloat16 [512, 256, 512], P('dev', None, 'side'), may hold values from -6 to 6
- new_key: bfloat16 [512, 512], P('dev', 'side'), may hold values from -15 to 15
- new_value: bfloat16 [512, 512], P('dev', 'side'), may hold values from -6 to 6
- cache_lengths: int32 [512], P('dev'), may hold values from 2 to 256, as said below
- hidden: bfloat16 [512, 4096], P('dev'), may hold values from -6 to 6
- norm_gain: bfloat16 [4096], replicated, may hold values from 0.099609375 to 1.8984375
- expert_ids: int32 [512, 8], P('dev'), may hold values from 0 to 15, all different within a row; in each aligned block of 32 rows (0 to 31, 32 to 63, ...) at most 32 rows name the same one
- router_probs: float32 [512, 8], P('dev'), may hold values from 0.02 to 1
- w_gate: bfloat16 [16, 4096, 1536], P('dev', None, 'side'), may hold values from -0.09375 to 0.09375
- w_up: bfloat16 [16, 4096, 1536], P('dev', None, 'side'), may hold values from -0.09375 to 0.09375
- w_down: bfloat16 [16, 1536, 4096], P('dev', 'side'), may hold values from -0.15625 to 0.15625
Outputs:
- context: bfloat16 [512, 8192], P('dev', 'side')
- moe_out: bfloat16 [512, 4096], P('dev')
The draws below stay inside these ranges and needn't reach their ends.
Inputs may be any that keep to these rules, and one draw needn't show every extreme that they name: `expert_ids`: in each aligned block of 32 rows (the rows of one dev index) no expert is named more than 32 times, a bound that some block reaches. `cache_lengths`: every aligned block of 32 tokens holds a token with 256 valid positions.
All inputs are finite; a program needn't handle non-finite values.
Results may differ from the reference program's by a relative error of at most 0.012.
Values may be sent and summed in bfloat16 or wider, within the bound.
No kernel may reach another device: no remote copies, remote signals or barrier semaphores. Data moves between devices by JAX's collectives and lax.ppermute only.
A program may use at most 128 MiB of HBM per device.

```python
import math
import jax
import jax.numpy as jnp
import numpy as np
from jax import lax

D = 4096
HEADS = 64
KV_HEADS = 4
HEAD_DIM = 128
FF = 1536
TOPK = 8
CACHE = 256
ROWS = 32
EXPERTS = 16
CAP = 32
TOKENS = 512
N_SIDE = 2
N_DEV = 16


def draw_queries(key, part):
    base = jnp.clip(jax.random.normal(jax.random.fold_in(key, 1), (TOKENS, HEADS * HEAD_DIM), jnp.float32), -5.0, 5.0)
    return base.astype(jnp.bfloat16)


def draw_cache_keys(key, part):
    base = jnp.clip(jax.random.normal(jax.random.fold_in(key, 2), (TOKENS, CACHE, KV_HEADS * HEAD_DIM), jnp.float32), -5.0, 5.0)
    return base.astype(jnp.bfloat16)


def draw_cache_lengths(key, part):
    drawn = jax.random.randint(jax.random.fold_in(key, 3), (TOKENS,), 2, CACHE + 1, dtype=jnp.int32)
    token_index = jnp.arange(TOKENS, dtype=jnp.int32)
    return jnp.where(token_index % ROWS == 5 % ROWS, CACHE, drawn).astype(jnp.int32)


def shard_levels(stream_key, dims, cuts, smallest, largest):
    loudness = 1.0
    for position, shards_of in cuts:
        draws = jax.random.uniform(jax.random.fold_in(jax.random.fold_in(stream_key, 6), position), (shards_of,), jnp.float32, smallest / len(cuts), largest / len(cuts))
        loudness = loudness * jnp.repeat(jnp.exp(draws), dims[position] // shards_of).reshape((-1,) + (1,) * (len(dims) - 1 - position))
    return loudness


def routed_block(rng, own, number, rows, count, top, reach, slope):
    ranking = jax.random.permutation(rng, count)
    heavy_load, ordinary = shares(count, rows * top, reach, slope, True), shares(count, rows * top, reach, slope, False)
    places = jnp.arange(count)

    def named(tallies, turn):
        used = int((tallies > 0).sum())
        fixed = max(1, used // 4)
        moved = fixed + (places - fixed + turn * (used - fixed)) % max(1, count - fixed)
        return jnp.zeros((count,), jnp.int32).at[ranking[jnp.where(places < fixed, places, moved)]].set(jnp.asarray(tallies, jnp.int32))

    tallies = jnp.where(number % 4 == 0, named(heavy_load, number // 4), named(ordinary, number - number // 4 - 1))
    mixed = jax.random.permutation(jax.random.fold_in(own, 3), count)
    source_of, sink = mixed[0:count // 2 * 2:2], mixed[1:count // 2 * 2:2]
    margin = jnp.minimum(tallies[source_of] - 1, reach - tallies[sink]) // 2
    margin = jnp.where((source_of == ranking[0]) | (sink == ranking[0]) | (tallies[sink] == 0), 0, jnp.maximum(margin, 0))
    moved = jax.random.randint(jax.random.fold_in(own, 4), (count // 2,), 0, 1 << 20) % (margin + 1)
    tallies = tallies.at[source_of].add(-moved).at[sink].add(moved)
    items = jnp.searchsorted(jnp.cumsum(tallies), jnp.arange(rows * top), side="right").astype(jnp.int32)
    listing = items.reshape(top, rows).T
    listing = listing[jax.random.permutation(jax.random.fold_in(own, 1), rows)]
    turn = jax.random.randint(jax.random.fold_in(own, 2), (rows, 1), 0, top)
    return jnp.take_along_axis(listing, (jnp.arange(top)[None, :] + turn) % top, axis=1)


def shares(number_of, total, limit, skew, full):
    weights = [(1 << 20) // math.isqrt(grade ** skew) + 1 for grade in range(1, number_of + 1)]
    largest = limit if full else min(limit, max(-(-total // number_of), total * weights[0] // sum(weights)))
    least = 1 if total - largest >= number_of - 1 else 0
    given, rest = [largest] + [least] * (number_of - 1), total - largest - least * (number_of - 1)
    while rest > 0:
        movable = [i for i in range(1, number_of) if given[i] < largest] or [i for i in range(1, number_of) if given[i] < limit]
        pool, budget = sum([weights[i] for i in movable]), rest
        for i in movable:
            more = min(limit - given[i], max(1, budget * weights[i] // pool), rest)
            given[i] = given[i] + more
            rest = rest - more
    return np.array(given)


def noise(key, shape, deviation, limit, pieces=(), kind=jnp.bfloat16):
    values = jax.random.normal(key, shape, jnp.float32) * deviation
    if len(pieces) > 0:
        values = shard_levels(key, shape, pieces, -0.22, 0.18) * values
    return jnp.clip(values, min=-limit, max=limit).astype(kind)


def setup_inputs(seed: int = 0) -> dict:
    splits = jax.random.split(jax.random.key(seed), 14)
    queries = draw_queries(jax.random.fold_in(splits[13], 71), 0)
    cache_keys = draw_cache_keys(jax.random.fold_in(splits[13], 71), 0)
    cache_values = noise(splits[2], (TOKENS, CACHE, KV_HEADS * HEAD_DIM), 1.0, 6.0, ((0, 16), (2, 2)))
    new_key = noise(splits[3], (TOKENS, KV_HEADS * HEAD_DIM), 2.5, 15.0, ((0, 16), (1, 2)))
    new_value = noise(splits[4], (TOKENS, KV_HEADS * HEAD_DIM), 1.0, 6.0, ((0, 16), (1, 2)))
    cache_lengths = draw_cache_lengths(jax.random.fold_in(splits[13], 71), 0)
    hidden = noise(splits[6], (TOKENS, D), 1.0, 6.0, ((0, 16),))
    norm_gain = jnp.clip(1.0 + 0.18 * jax.random.normal(splits[7], (D,), jnp.float32), 0.099609375, 1.8984375).astype(jnp.bfloat16)
    expert_ids_keys = jax.random.split(jax.random.fold_in(splits[8], 1), TOKENS // ROWS)
    expert_ids_turns = jax.random.permutation(jax.random.fold_in(splits[8], 3), TOKENS // ROWS)
    expert_ids = jax.vmap(lambda own, number: routed_block(jax.random.fold_in(splits[8], 2), own, number, ROWS, EXPERTS, TOPK, CAP, 2))(expert_ids_keys, expert_ids_turns).reshape((TOKENS, TOPK))
    router_probs = jnp.clip(jnp.exp(math.log(1.0) - 3.912023 * jax.random.uniform(splits[9], (TOKENS, TOPK), jnp.float32) ** shard_levels(splits[9], (TOKENS, TOPK), ((0, 16),), -0.2, 0.2)), 0.02, 1.0)
    w_gate = noise(splits[10], (EXPERTS, D, FF), D ** -0.5, 0.09375, ((0, 16), (2, 2)))
    w_up = noise(splits[11], (EXPERTS, D, FF), D ** -0.5, 0.09375, ((0, 16), (2, 2)))
    w_down = noise(splits[12], (EXPERTS, FF, D), FF ** -0.5, 0.15625, ((0, 16), (1, 2)))
    return {"queries": queries, "cache_keys": cache_keys, "cache_values": cache_values, "new_key": new_key, "new_value": new_value, "cache_lengths": cache_lengths, "hidden": hidden, "norm_gain": norm_gain, "expert_ids": expert_ids, "router_probs": router_probs, "w_gate": w_gate, "w_up": w_up, "w_down": w_down}


def route_onehot(block_ids, expert_count, capacity):
    flat_ids = block_ids.reshape(-1)
    expert_hot = (flat_ids[:, None] == jnp.arange(expert_count, dtype=jnp.int32)[None, :]).astype(jnp.int32)
    earlier = jnp.cumsum(expert_hot, axis=0) - expert_hot
    slot_rank = lax.optimization_barrier(jnp.sum(earlier * expert_hot, axis=1))
    slot_hot = (slot_rank[:, None] == jnp.arange(capacity, dtype=jnp.int32)[None, :]).astype(jnp.float32)
    route_hot = expert_hot.astype(jnp.float32)[:, :, None] * slot_hot[:, None, :]
    return route_hot.reshape(block_ids.shape[0], block_ids.shape[1], expert_count, capacity)

def attend_block(block_args):
    query_block, key_block, value_block, key_new, value_new, block_lengths = block_args
    row_count = query_block.shape[0]
    per_group = HEADS // KV_HEADS
    score_scale = HEAD_DIM ** (-0.5)
    query_heads = query_block.astype(jnp.float32).reshape(row_count, KV_HEADS, per_group, HEAD_DIM)
    key_heads = key_block.astype(jnp.float32).reshape(row_count, CACHE, KV_HEADS, HEAD_DIM)
    value_heads = value_block.astype(jnp.float32).reshape(row_count, CACHE, KV_HEADS, HEAD_DIM)
    scores = jnp.einsum('tgqd,tlgd->tgql', query_heads, key_heads) * score_scale
    own_key = key_new.astype(jnp.float32).reshape(row_count, KV_HEADS, HEAD_DIM)
    own_score = jnp.einsum('tgqd,tgd->tgq', query_heads, own_key) * score_scale
    visible = jnp.arange(CACHE, dtype=jnp.int32)[None, :] < block_lengths[:, None]
    scores = jnp.where(visible[:, None, None, :], scores, -1e+30)
    top_score = jnp.maximum(lax.optimization_barrier(jnp.max(scores, axis=3)), own_score)
    exp_scores = jnp.exp(scores - top_score[..., None])
    own_exp = jnp.exp(own_score - top_score)
    denominator = lax.optimization_barrier(jnp.sum(exp_scores, axis=3)) + own_exp
    attn_weights = (exp_scores / denominator[..., None]).astype(jnp.bfloat16)
    own_prob = (own_exp / denominator).astype(jnp.bfloat16)
    combined = jnp.einsum('tgql,tlgd->tgqd', attn_weights.astype(jnp.float32), value_heads)
    own_value = value_new.astype(jnp.float32).reshape(row_count, KV_HEADS, 1, HEAD_DIM)
    combined = combined + own_prob.astype(jnp.float32)[..., None] * own_value
    return combined.reshape(row_count, HEADS * HEAD_DIM).astype(jnp.bfloat16)

def by_block(array):
    return array.reshape((N_DEV, ROWS) + array.shape[1:])

def reference(queries, cache_keys, cache_values, new_key, new_value, cache_lengths, hidden, norm_gain, expert_ids, router_probs, w_gate, w_up, w_down):
    context = lax.map(attend_block, (by_block(queries), by_block(cache_keys), by_block(cache_values), by_block(new_key), by_block(new_value), by_block(cache_lengths)))
    context = context.reshape(TOKENS, HEADS * HEAD_DIM)
    gate_share = router_probs / lax.optimization_barrier(jnp.sum(router_probs, axis=1, keepdims=True))
    hidden_wide = hidden.astype(jnp.float32)
    inverse = lax.rsqrt(lax.optimization_barrier(jnp.mean(hidden_wide * hidden_wide, axis=1, keepdims=True)) + 1e-06)
    normed = (hidden_wide * inverse * norm_gain.astype(jnp.float32)[None, :]).astype(jnp.bfloat16)
    block_ids = expert_ids.reshape(N_DEV, ROWS, TOPK)
    block_hot = jax.vmap(route_onehot, in_axes=(0, None, None))(block_ids, EXPERTS, CAP)
    slot_hot = lax.optimization_barrier(jnp.sum(block_hot, axis=2))
    slot_gate = lax.optimization_barrier(jnp.sum(block_hot * gate_share.reshape(N_DEV, ROWS, TOPK)[..., None, None], axis=2))
    buffers = jnp.einsum('nrec,nrd->encd', slot_hot, normed.astype(jnp.float32).reshape(N_DEV, ROWS, D)).astype(jnp.bfloat16)
    expert_gates = jnp.transpose(slot_gate, (2, 0, 1, 3))
    half_width = FF // N_SIDE

    def expert_step(running, expert_items):
        expert_rows, gate_weight, up_weight, down_weight, expert_gate = expert_items
        flat_rows = expert_rows.reshape(N_DEV * CAP, D)
        gate_act = jnp.dot(flat_rows, gate_weight, preferred_element_type=jnp.float32)
        up_act = jnp.dot(flat_rows, up_weight, preferred_element_type=jnp.float32)
        activation = (jax.nn.silu(gate_act) * up_act).astype(jnp.bfloat16)
        summed = jnp.zeros((N_DEV * CAP, D), jnp.float32)
        for half_index in range(N_SIDE):
            low = half_index * half_width
            partial_value = jnp.dot(activation[:, low:low + half_width], down_weight[low:low + half_width], preferred_element_type=jnp.float32).astype(jnp.bfloat16)
            summed = summed + partial_value.astype(jnp.float32)
        summed = summed.reshape(N_DEV, CAP, D)
        running = running + jnp.einsum('nrc,ncd->nrd', expert_gate, summed, precision=lax.Precision.HIGHEST)
        return (running, None)
    running, _ = lax.scan(expert_step, jnp.zeros((N_DEV, ROWS, D), jnp.float32), (buffers, w_gate, w_up, w_down, expert_gates))
    moe_out = running.reshape(TOKENS, D).astype(jnp.bfloat16)
    return (context, moe_out)
```

```python
import jax
import jax.numpy as jnp
from jax import lax
from jax.experimental import pallas as pl
from jax.experimental.pallas import tpu as pltpu
from jax.sharding import PartitionSpec as P

HEADS = 64
KV_HEADS = 4
HEAD_DIM = 128


def attend_local(queries, cache_keys, cache_values, new_key, new_value, cache_lengths):
    row_count = queries.shape[0]
    cache_len = cache_keys.shape[1]
    groups = cache_keys.shape[2] // HEAD_DIM
    per_group = HEADS // KV_HEADS
    score_scale = HEAD_DIM ** (-0.5)
    query_heads = queries.reshape(row_count, groups, per_group, HEAD_DIM)
    key_heads = cache_keys.reshape(row_count, cache_len, groups, HEAD_DIM)
    value_heads = cache_values.reshape(row_count, cache_len, groups, HEAD_DIM)
    scores = (
        jnp.einsum("tgqd,tlgd->tgql", query_heads, key_heads, preferred_element_type=jnp.float32)
        * score_scale
    )
    own_key = new_key.reshape(row_count, groups, HEAD_DIM)
    own_score = (
        jnp.einsum("tgqd,tgd->tgq", query_heads, own_key, preferred_element_type=jnp.float32)
        * score_scale
    )
    visible = jnp.arange(cache_len, dtype=jnp.int32)[None, :] < cache_lengths[:, None]
    scores = jnp.where(visible[:, None, None, :], scores, -1e30)
    top_score = jnp.maximum(jnp.max(scores, axis=3), own_score)
    exp_scores = jnp.exp(scores - top_score[..., None])
    own_exp = jnp.exp(own_score - top_score)
    denominator = jnp.sum(exp_scores, axis=3) + own_exp
    attn_weights = (exp_scores / denominator[..., None]).astype(jnp.bfloat16)
    own_prob = (own_exp / denominator).astype(jnp.bfloat16)
    combined = jnp.einsum(
        "tgql,tlgd->tgqd", attn_weights, value_heads, preferred_element_type=jnp.float32
    )
    own_value = new_value.reshape(row_count, groups, 1, HEAD_DIM).astype(jnp.float32)
    combined = combined + own_prob.astype(jnp.float32)[..., None] * own_value
    return combined.reshape(row_count, groups * per_group * HEAD_DIM).astype(jnp.bfloat16)


def norm_kernel(side_ref, hidden_ref, gain_ref, ids_ref, probs_ref, rows_ref, half_ref):
    features = hidden_ref.shape[1]
    row_count = hidden_ref.shape[0]
    lanes = rows_ref.shape[1] - features
    wide = hidden_ref[...].astype(jnp.float32)
    inverse = lax.rsqrt(jnp.mean(wide * wide, axis=1, keepdims=True) + 1e-06)
    normed = wide * inverse * gain_ref[...].astype(jnp.float32)
    probs = probs_ref[...]
    share = probs / jnp.sum(probs, axis=1, keepdims=True)
    ids = ids_ref[...]
    lane = lax.broadcasted_iota(jnp.int32, (row_count, lanes), 1)
    half_lanes = lanes // 2
    expert_of = jnp.where(lane < half_lanes, lane, lane - half_lanes)
    gates = jnp.zeros((row_count, lanes), jnp.float32)
    for k in range(ids.shape[1]):
        gates = gates + jnp.where(expert_of == ids[:, k : k + 1], share[:, k : k + 1], 0.0)
    coarse = gates.astype(jnp.bfloat16).astype(jnp.float32)
    gates = jnp.where(lane < half_lanes, coarse, gates - coarse)
    whole = jnp.concatenate([normed, gates], axis=1)
    half = row_count // 2
    first = side_ref[0] == 0
    mine = jnp.where(first, whole[:half], whole[half:]).astype(jnp.bfloat16)
    other = jnp.where(first, whole[half:], whole[:half]).astype(jnp.bfloat16)
    rows_ref[:half] = mine
    rows_ref[half:] = other
    half_ref[...] = mine


def normed_rows(hidden, norm_gain, expert_ids, router_probs, experts):
    row_count, features = hidden.shape
    lanes = 128 * (-(-2 * experts // 128))
    side = lax.axis_index("side").astype(jnp.int32).reshape(1)
    width = features + lanes
    vmem = pl.BlockSpec(memory_space=pltpu.VMEM)
    return pl.pallas_call(
        norm_kernel,
        in_specs=[pl.BlockSpec(memory_space=pltpu.SMEM), vmem, vmem, vmem, vmem],
        out_specs=(vmem, vmem),
        out_shape=(
            jax.ShapeDtypeStruct((row_count, width), jnp.bfloat16),
            jax.ShapeDtypeStruct((row_count // 2, width), jnp.bfloat16),
        ),
        name="norm_and_gates",
    )(side, hidden, norm_gain.reshape(1, features), expert_ids, router_probs)


def expert_kernel(
    expert_ref, own_ref, other_ref, gate_ref, up_ref, down_ref, own_out, other_out, total
):
    step = pl.program_id(0)
    features = gate_ref.shape[1]
    rows = own_ref.shape[0]
    x = jnp.concatenate([own_ref[:, :features], other_ref[:, :features]], axis=0)
    tail = jnp.concatenate([own_ref[:, features:], other_ref[:, features:]], axis=0)
    lanes = tail.shape[1]
    lane = lax.broadcasted_iota(jnp.int32, tail.shape, 1)
    mine = (lane == expert_ref[0]) | (lane == expert_ref[0] + lanes // 2)
    share = jnp.sum(jnp.where(mine, tail.astype(jnp.float32), 0.0), axis=1, keepdims=True)
    gate_act = jnp.dot(x, gate_ref[0], preferred_element_type=jnp.float32)
    up_act = jnp.dot(x, up_ref[0], preferred_element_type=jnp.float32)
    activation = (jax.nn.silu(gate_act) * up_act * share).astype(jnp.bfloat16)
    part = jnp.dot(activation, down_ref[0], preferred_element_type=jnp.float32)

    @pl.when(step == 0)
    def _():
        total[...] = part

    @pl.when(step > 0)
    def _():
        total[...] += part

    @pl.when(step == pl.num_programs(0) - 1)
    def _():
        own_out[...] = total[:rows].astype(jnp.bfloat16)
        other_out[...] = total[rows:].astype(jnp.bfloat16)


def expert_rows(own, other, w_gate, w_up, w_down):
    rows, width = own.shape
    _, features, hidden_units = w_gate.shape
    chunk = 256
    expert = lax.axis_index("dev").astype(jnp.int32).reshape(1)
    whole = pl.BlockSpec((rows, width), lambda j: (0, 0))
    out = pl.BlockSpec((rows, features), lambda j: (0, 0))
    return pl.pallas_call(
        expert_kernel,
        grid=(hidden_units // chunk,),
        in_specs=[
            pl.BlockSpec(memory_space=pltpu.SMEM),
            whole,
            whole,
            pl.BlockSpec((1, features, chunk), lambda j: (0, 0, j)),
            pl.BlockSpec((1, features, chunk), lambda j: (0, 0, j)),
            pl.BlockSpec((1, chunk, features), lambda j: (0, j, 0)),
        ],
        out_specs=(out, out),
        out_shape=(jax.ShapeDtypeStruct((rows, features), jnp.bfloat16),) * 2,
        scratch_shapes=[pltpu.VMEM((2 * rows, features), jnp.float32)],
        compiler_params=pltpu.CompilerParams(
            dimension_semantics=("arbitrary",), vmem_limit_bytes=50 * 1024 * 1024
        ),
        name="expert_rows",
    )(expert, own, other, w_gate, w_up, w_down)


def add(*parts):
    total = parts[0].astype(jnp.float32)
    for part in parts[1:]:
        total = total + part.astype(jnp.float32)
    return total


def add_rounded(*parts):
    return add(*parts).astype(jnp.bfloat16)


def per_device(
    queries,
    cache_keys,
    cache_values,
    new_key,
    new_value,
    cache_lengths,
    hidden,
    norm_gain,
    expert_ids,
    router_probs,
    w_gate,
    w_up,
    w_down,
):
    devices = lax.axis_size("dev")
    planes = devices // 4
    experts = w_gate.shape[0] * devices

    def over(bit):
        return lambda a: lax.ppermute(a, "dev", [(d, d ^ bit) for d in range(devices)])

    core, across = over(1), over(2)
    sides = lambda a: lax.ppermute(a, "side", [(0, 1), (1, 0)])

    own_rows, own_half = normed_rows(hidden, norm_gain, expert_ids, router_probs, experts)
    half = own_half.shape[0]
    arrived = {i: over(4 * i)(own_half) for i in range(1, planes)}
    context = attend_local(queries, cache_keys, cache_values, new_key, new_value, cache_lengths)
    blocks = {0: [own_rows, across(own_rows)]}
    for i in range(1, planes):
        mine = arrived[i]
        beside, facing = across(mine), sides(mine)
        diagonal = sides(beside) if i % 4 != 3 else across(facing)
        blocks[i] = [mine, facing, beside, diagonal]

    reduced = {}
    for first in range(0, planes, 2):
        group = [first, first + 1]
        stack = jnp.concatenate(blocks[first] + blocks[first + 1], axis=0)
        own_out, other_out = expert_rows(stack, core(stack), w_gate, w_up, w_down)
        merged = add_rounded(own_out, core(other_out))
        for place, i in enumerate(group):
            four = merged[place * 4 * half : (place + 1) * 4 * half]
            if i % 4 in (0, 3):
                pair = add_rounded(four[: 2 * half], across(four[2 * half :]))
                parts = (pair[:half], sides(pair[half:]))
            else:
                mine, facing, beside, diagonal = (four[j * half : (j + 1) * half] for j in range(4))
                got = sides(jnp.concatenate([facing, diagonal], axis=0))
                mine = add(mine, got[:half])
                parts = (mine, across(add_rounded(beside, got[half:])))
            if i == 0:
                reduced[i] = add(*parts)
            else:
                reduced[i] = over(4 * i)(add_rounded(*parts))
    total = add_rounded(*(reduced[i] for i in range(planes)))
    partner = sides(total)
    first = lax.axis_index("side") == 0
    moe_out = jnp.concatenate(
        [jnp.where(first, total, partner), jnp.where(first, partner, total)], axis=0
    )
    return (context, moe_out)


def solution(mesh):
    in_specs = (
        P("dev", "side"),
        P("dev", None, "side"),
        P("dev", None, "side"),
        P("dev", "side"),
        P("dev", "side"),
        P("dev"),
        P("dev", None),
        P(),
        P("dev", None),
        P("dev", None),
        P("dev", None, "side"),
        P("dev", None, "side"),
        P("dev", "side", None),
    )
    out_specs = (P("dev", "side"), P("dev", None))
    return jax.shard_map(
        per_device, mesh=mesh, in_specs=in_specs, out_specs=out_specs, check_vma=False
    )
```

```python
import functools

import jax
import jax.numpy as jnp
from jax import lax
from jax.experimental import pallas as pl
from jax.experimental.pallas import tpu as pltpu
from jax.sharding import PartitionSpec as P

HEADS = 64
KV_HEADS = 4
HEAD_DIM = 128


def in_hbm(*arrays):
    return [pltpu.with_memory_space_constraint(a, pltpu.HBM) for a in arrays]


def attend_kernel(
    lengths_ref,
    query_src,
    key_src,
    value_src,
    new_key_src,
    new_value_src,
    *rest,
    chunk,
    together,
):
    weight_srcs, context_ref, weight_refs = rest[:3], rest[3], rest[4:7]
    queries, keys, values, new_key, new_value, by_token, mixed, sems = rest[7:]
    row_count, cache_len, width = keys.shape
    groups = width // HEAD_DIM
    per_group = HEADS // KV_HEADS
    heads = groups * per_group
    score_scale = HEAD_DIM ** (-0.5)
    small = [
        pltpu.make_async_copy(source, target, sems.at[0, j])
        for j, (source, target) in enumerate(
            ((query_src, queries), (new_key_src, new_key), (new_value_src, new_value))
        )
    ]
    cached = [
        [
            pltpu.make_async_copy(
                source.at[pl.ds(low, chunk)], target.at[pl.ds(low, chunk)], sems.at[1 + j, place]
            )
            for j, (source, target) in enumerate(((key_src, keys), (value_src, values)))
        ]
        for place, low in enumerate(range(0, row_count, chunk))
    ]
    weights = [
        pltpu.make_async_copy(source, target, sems.at[3, j])
        for j, (source, target) in enumerate(zip(weight_srcs, weight_refs))
    ]
    for copy in small + sum(cached, []) + weights:
        copy.start()
    for copy in small:
        copy.wait()
    for head in range(heads):
        columns = slice(head * HEAD_DIM, (head + 1) * HEAD_DIM)
        by_token[pl.ds(head, row_count, stride=heads), :] = queries[:, columns].astype(jnp.float32)
    group_of = lax.broadcasted_iota(jnp.int32, (heads, HEAD_DIM), 0) // per_group
    position = lax.broadcasted_iota(jnp.int32, (heads, cache_len), 1)
    own_keys = new_key[...].astype(jnp.float32)
    own_values = new_value[...].astype(jnp.float32)
    for place, low in enumerate(range(0, row_count, chunk)):
        for copy in cached[place]:
            copy.wait()
        for first in range(low, low + chunk, together):
            tokens = range(first, first + together)
            spread, scores, own_score = [], [], []
            for token in tokens:
                query = by_token[token * heads : (token + 1) * heads, :]
                spread = jnp.concatenate(
                    [jnp.where(group_of == g, query, 0.0) for g in range(groups)], axis=1
                )
                score = lax.dot_general(
                    spread.astype(jnp.bfloat16),
                    keys[token],
                    (((1,), (1,)), ((), ())),
                    preferred_element_type=jnp.float32,
                )
                scores.append(
                    jnp.where(position < lengths_ref[token], score * score_scale, -1e30)
                )
                own_score.append(
                    jnp.sum(spread * own_keys[token : token + 1], axis=1, keepdims=True)
                )
            scores = jnp.concatenate(scores, axis=0)
            own_score = jnp.concatenate(own_score, axis=0) * score_scale
            top_score = jnp.maximum(jnp.max(scores, axis=1, keepdims=True), own_score)
            exp_scores = jnp.exp(scores - top_score)
            own_exp = jnp.exp(own_score - top_score)
            inverse = 1.0 / (jnp.sum(exp_scores, axis=1, keepdims=True) + own_exp)
            attn_weights = (exp_scores * inverse).astype(jnp.bfloat16)
            own_prob = (own_exp * inverse).astype(jnp.bfloat16).astype(jnp.float32)
            for place_of, token in enumerate(tokens):
                rows = slice(place_of * heads, (place_of + 1) * heads)
                combined = jnp.dot(
                    attn_weights[rows], values[token], preferred_element_type=jnp.float32
                )
                combined = combined + own_prob[rows] * own_values[token : token + 1]
                picked = combined[:, :HEAD_DIM]
                for g in range(1, groups):
                    columns = slice(g * HEAD_DIM, (g + 1) * HEAD_DIM)
                    picked = jnp.where(group_of == g, combined[:, columns], picked)
                mixed[token * heads : (token + 1) * heads, :] = picked
    for head in range(heads):
        columns = slice(head * HEAD_DIM, (head + 1) * HEAD_DIM)
        context_ref[:, columns] = mixed[pl.ds(head, row_count, stride=heads), :].astype(
            jnp.bfloat16
        )
    for copy in weights:
        copy.wait()


def attend_and_stage(
    queries, cache_keys, cache_values, new_key, new_value, cache_lengths, weights
):
    row_count, width = queries.shape
    heads = width // HEAD_DIM
    vmem, hbm = pl.BlockSpec(memory_space=pltpu.VMEM), pl.BlockSpec(memory_space=pltpu.HBM)
    held = (queries, cache_keys, cache_values, new_key, new_value)
    chunk = 8
    out = pl.pallas_call(
        functools.partial(attend_kernel, chunk=chunk, together=4),
        in_specs=[pl.BlockSpec(memory_space=pltpu.SMEM)] + [hbm] * 8,
        out_specs=[vmem] * 4,
        out_shape=[jax.ShapeDtypeStruct(queries.shape, queries.dtype)]
        + [pltpu.VMEM(w.shape, w.dtype) for w in weights],
        scratch_shapes=[pltpu.VMEM(a.shape, a.dtype) for a in held]
        + [pltpu.VMEM((row_count * heads, HEAD_DIM), jnp.float32)] * 2
        + [pltpu.SemaphoreType.DMA((4, max(4, row_count // chunk)))],
        compiler_params=pltpu.CompilerParams(vmem_limit_bytes=16 * 1024 * 1024),
        name="attend_and_stage",
    )(cache_lengths, *in_hbm(*held, *weights))
    return out[0], out[1:]


def norm_kernel(side_ref, *refs):
    sources, (rows_ref, half_ref), held, sems = refs[:4], refs[4:6], refs[6:10], refs[10]
    copies = [
        pltpu.make_async_copy(source, target, sems.at[j])
        for j, (source, target) in enumerate(zip(sources, held))
    ]
    for copy in copies:
        copy.start()
    for copy in copies:
        copy.wait()
    hidden_ref, gain_ref, ids_ref, probs_ref = held
    features = hidden_ref.shape[1]
    row_count = hidden_ref.shape[0]
    lanes = rows_ref.shape[1] - features
    wide = hidden_ref[...].astype(jnp.float32)
    inverse = lax.rsqrt(jnp.mean(wide * wide, axis=1, keepdims=True) + 1e-06)
    normed = wide * inverse * gain_ref[...].astype(jnp.float32).reshape(1, features)
    probs = probs_ref[...]
    share = probs / jnp.sum(probs, axis=0, keepdims=True)
    ids = ids_ref[...]
    place = lax.broadcasted_iota(jnp.int32, (lanes, row_count), 0)
    half_lanes = lanes // 2
    expert_of = jnp.where(place < half_lanes, place, place - half_lanes)
    gates = jnp.zeros((lanes, row_count), jnp.float32)
    for k in range(ids.shape[0]):
        gates = gates + jnp.where(expert_of == ids[k : k + 1], share[k : k + 1], 0.0)
    coarse = gates.astype(jnp.bfloat16).astype(jnp.float32)
    gates = jnp.where(place < half_lanes, coarse, gates - coarse).T
    half = row_count // 2
    first = side_ref[0] == 0

    def store(columns, values):
        values = values.astype(jnp.bfloat16)
        mine = jnp.where(first, values[:half], values[half:])
        rows_ref[:half, columns] = mine
        rows_ref[half:, columns] = jnp.where(first, values[half:], values[:half])
        half_ref[:, columns] = mine

    store(slice(0, features), normed)
    store(slice(features, features + lanes), gates)


def normed_rows(hidden, norm_gain, expert_ids, router_probs, experts):
    row_count, features = hidden.shape
    lanes = 128 * (-(-2 * experts // 128))
    side = lax.axis_index("side").astype(jnp.int32).reshape(1)
    width = features + lanes
    vmem, hbm = pl.BlockSpec(memory_space=pltpu.VMEM), pl.BlockSpec(memory_space=pltpu.HBM)
    held = (hidden, norm_gain, expert_ids.T, router_probs.T)
    return pl.pallas_call(
        norm_kernel,
        in_specs=[pl.BlockSpec(memory_space=pltpu.SMEM)] + [hbm] * 4,
        out_specs=(vmem, vmem),
        out_shape=(
            jax.ShapeDtypeStruct((row_count, width), jnp.bfloat16),
            jax.ShapeDtypeStruct((row_count // 2, width), jnp.bfloat16),
        ),
        scratch_shapes=[pltpu.VMEM(a.shape, a.dtype) for a in held]
        + [pltpu.SemaphoreType.DMA((4,))],
        compiler_params=pltpu.CompilerParams(vmem_limit_bytes=8 * 1024 * 1024),
        name="norm_and_gates",
    )(side, *in_hbm(*held))


def expert_kernel(
    expert_ref,
    early_own_ref,
    early_other_ref,
    late_own_ref,
    late_other_ref,
    gate_ref,
    up_ref,
    down_ref,
    own_out,
    other_out,
    activation,
):
    features = gate_ref.shape[1]
    rows = own_out.shape[0]
    sources = (early_own_ref, late_own_ref, early_other_ref, late_other_ref)
    x = jnp.concatenate([ref[:, :features] for ref in sources], axis=0)
    tail = jnp.concatenate([ref[:, features:] for ref in sources], axis=0)
    lanes = tail.shape[1]
    lane = lax.broadcasted_iota(jnp.int32, tail.shape, 1)
    mine = (lane == expert_ref[0]) | (lane == expert_ref[0] + lanes // 2)
    share = jnp.sum(jnp.where(mine, tail.astype(jnp.float32), 0.0), axis=1, keepdims=True)
    for low in range(0, gate_ref.shape[2], 256):
        units = slice(low, low + 256)
        gate_act = jnp.dot(x, gate_ref[0, :, units], preferred_element_type=jnp.float32)
        up_act = jnp.dot(x, up_ref[0, :, units], preferred_element_type=jnp.float32)
        activation[:, units] = (jax.nn.silu(gate_act) * up_act * share).astype(jnp.bfloat16)
    hidden_units = activation[...]
    for low in range(0, features, 1024):
        columns = slice(low, low + 1024)
        part = jnp.dot(
            hidden_units, down_ref[0, :, columns], preferred_element_type=jnp.float32
        ).astype(jnp.bfloat16)
        own_out[:, columns] = part[:rows]
        other_out[:, columns] = part[rows:]


def expert_rows(early_own, early_other, late_own, late_other, weights):
    rows = early_own.shape[0] + late_own.shape[0]
    _, features, hidden_units = weights[0].shape
    expert = lax.axis_index("dev").astype(jnp.int32).reshape(1)
    vmem = pl.BlockSpec(memory_space=pltpu.VMEM)
    return pl.pallas_call(
        expert_kernel,
        in_specs=[pl.BlockSpec(memory_space=pltpu.SMEM)] + [vmem] * 7,
        out_specs=(vmem, vmem),
        out_shape=(jax.ShapeDtypeStruct((rows, features), jnp.bfloat16),) * 2,
        scratch_shapes=[pltpu.VMEM((2 * rows, hidden_units), jnp.bfloat16)],
        compiler_params=pltpu.CompilerParams(vmem_limit_bytes=24 * 1024 * 1024),
        name="expert_rows",
    )(
        expert,
        early_own,
        early_other,
        late_own,
        late_other,
        *(pltpu.with_memory_space_constraint(w, pltpu.VMEM) for w in weights),
    )


def add(*parts):
    total = parts[0].astype(jnp.float32)
    for part in parts[1:]:
        total = total + part.astype(jnp.float32)
    return total


def add_rounded(*parts):
    return add(*parts).astype(jnp.bfloat16)


def per_device(
    queries,
    cache_keys,
    cache_values,
    new_key,
    new_value,
    cache_lengths,
    hidden,
    norm_gain,
    expert_ids,
    router_probs,
    w_gate,
    w_up,
    w_down,
):
    devices = lax.axis_size("dev")
    planes = devices // 4
    experts = w_gate.shape[0] * devices

    def over(bit):
        return lambda a: lax.ppermute(a, "dev", [(d, d ^ bit) for d in range(devices)])

    core, across = over(1), over(2)
    sides = lambda a: lax.ppermute(a, "side", [(0, 1), (1, 0)])

    own_rows, own_half = normed_rows(hidden, norm_gain, expert_ids, router_probs, experts)
    half = own_half.shape[0]
    arrived = {i: over(4 * i)(own_half) for i in range(1, planes)}
    beside_own = across(own_rows)
    context, weights = attend_and_stage(
        queries,
        cache_keys,
        cache_values,
        new_key,
        new_value,
        cache_lengths,
        (w_gate, w_up, w_down),
    )
    far = range(2, planes)
    context, weights, waited = lax.optimization_barrier(
        (context, weights, [arrived[i] for i in far])
    )
    arrived.update(zip(far, waited))

    blocks = {}
    for first in range(planes - 2, -1, -2):
        early, late = [], []
        for i in (first, first + 1):
            if i == 0:
                early += [own_rows, beside_own]
                continue
            mine = arrived[i]
            beside, facing = across(mine), sides(mine)
            early += [mine, facing, beside]
            late.append(sides(beside) if i % 4 != 3 else across(facing))
        early, late = jnp.concatenate(early, axis=0), jnp.concatenate(late, axis=0)
        blocks[first] = (early, core(early), late, core(late))

    reduced = {}
    for first in range(planes - 2, -1, -2):
        own_out, other_out = expert_rows(*blocks[first], weights)
        merged = add_rounded(own_out, core(other_out))
        rows = [merged[j * half : (j + 1) * half] for j in range(8)]
        rows = (rows[:4], rows[4:]) if first == 0 else (rows[:3] + rows[6:7], rows[3:6] + rows[7:])
        for i, (mine, facing, beside, diagonal) in zip((first, first + 1), rows):
            if i % 4 in (0, 3):
                got = across(jnp.concatenate([beside, diagonal], axis=0))
                parts = (add(mine, got[:half]), sides(add_rounded(facing, got[half:])))
            else:
                got = sides(jnp.concatenate([facing, diagonal], axis=0))
                parts = (add(mine, got[:half]), across(add_rounded(beside, got[half:])))
            if i == 0:
                reduced[i] = add(*parts)
            else:
                reduced[i] = over(4 * i)(add_rounded(*parts))
    total = add_rounded(*(reduced[i] for i in range(planes)))
    partner = sides(total)
    first = lax.axis_index("side") == 0
    moe_out = jnp.concatenate(
        [jnp.where(first, total, partner), jnp.where(first, partner, total)], axis=0
    )
    return (context, moe_out)


def solution(mesh):
    in_specs = (
        P("dev", "side"),
        P("dev", None, "side"),
        P("dev", None, "side"),
        P("dev", "side"),
        P("dev", "side"),
        P("dev"),
        P("dev", None),
        P(),
        P("dev", None),
        P("dev", None),
        P("dev", None, "side"),
        P("dev", None, "side"),
        P("dev", "side", None),
    )
    out_specs = (P("dev", "side"), P("dev", None))
    return jax.shard_map(
        per_device, mesh=mesh, in_specs=in_specs, out_specs=out_specs, check_vma=False
    )
```

```python
import functools

import jax
import jax.numpy as jnp
from jax import lax
from jax.experimental import pallas as pl
from jax.experimental.pallas import tpu as pltpu
from jax.sharding import PartitionSpec as P

HEADS = 64
KV_HEADS = 4
HEAD_DIM = 128


def in_hbm(*arrays):
    return [pltpu.with_memory_space_constraint(a, pltpu.HBM) for a in arrays]


def attend_kernel(
    lengths_ref,
    query_src,
    key_src,
    value_src,
    new_key_src,
    new_value_src,
    *rest,
    start,
    chunk,
    together,
):
    staged = (len(rest) - 9) // 2
    weight_srcs, context_ref, weight_refs = (
        rest[:staged],
        rest[staged],
        rest[staged + 1 : 2 * staged + 1],
    )
    queries, keys, values, new_key, new_value, by_token, mixed, sems = rest[2 * staged + 1 :]
    row_count, cache_len, width = keys.shape
    groups = width // HEAD_DIM
    per_group = HEADS // KV_HEADS
    heads = groups * per_group
    score_scale = HEAD_DIM ** (-0.5)
    small = [
        pltpu.make_async_copy(source.at[pl.ds(start, row_count)], target, sems.at[0, j])
        for j, (source, target) in enumerate(
            ((query_src, queries), (new_key_src, new_key), (new_value_src, new_value))
        )
    ]
    cached = [
        [
            pltpu.make_async_copy(
                source.at[pl.ds(start + low, chunk)],
                target.at[pl.ds(low, chunk)],
                sems.at[1 + j, place],
            )
            for j, (source, target) in enumerate(((key_src, keys), (value_src, values)))
        ]
        for place, low in enumerate(range(0, row_count, chunk))
    ]
    weights = [
        pltpu.make_async_copy(source, target, sems.at[3, j])
        for j, (source, target) in enumerate(zip(weight_srcs, weight_refs))
    ]
    for copy in small + sum(cached, []) + weights:
        copy.start()
    for copy in small:
        copy.wait()
    for head in range(heads):
        columns = slice(head * HEAD_DIM, (head + 1) * HEAD_DIM)
        by_token[pl.ds(head, row_count, stride=heads), :] = queries[:, columns].astype(jnp.float32)
    group_of = lax.broadcasted_iota(jnp.int32, (heads, HEAD_DIM), 0) // per_group
    position = lax.broadcasted_iota(jnp.int32, (heads, cache_len), 1)
    own_keys = new_key[...].astype(jnp.float32)
    own_values = new_value[...].astype(jnp.float32)
    for place, low in enumerate(range(0, row_count, chunk)):
        for copy in cached[place]:
            copy.wait()
        for first in range(low, low + chunk, together):
            tokens = range(first, first + together)
            spread, scores, own_score = [], [], []
            for token in tokens:
                query = by_token[token * heads : (token + 1) * heads, :]
                spread = jnp.concatenate(
                    [jnp.where(group_of == g, query, 0.0) for g in range(groups)], axis=1
                )
                score = lax.dot_general(
                    spread.astype(jnp.bfloat16),
                    keys[token],
                    (((1,), (1,)), ((), ())),
                    preferred_element_type=jnp.float32,
                )
                scores.append(
                    jnp.where(position < lengths_ref[start + token], score * score_scale, -1e30)
                )
                own_score.append(
                    jnp.sum(spread * own_keys[token : token + 1], axis=1, keepdims=True)
                )
            scores = jnp.concatenate(scores, axis=0)
            own_score = jnp.concatenate(own_score, axis=0) * score_scale
            top_score = jnp.maximum(jnp.max(scores, axis=1, keepdims=True), own_score)
            exp_scores = jnp.exp(scores - top_score)
            own_exp = jnp.exp(own_score - top_score)
            inverse = 1.0 / (jnp.sum(exp_scores, axis=1, keepdims=True) + own_exp)
            attn_weights = (exp_scores * inverse).astype(jnp.bfloat16)
            own_prob = (own_exp * inverse).astype(jnp.bfloat16).astype(jnp.float32)
            for place_of, token in enumerate(tokens):
                rows = slice(place_of * heads, (place_of + 1) * heads)
                combined = jnp.dot(
                    attn_weights[rows], values[token], preferred_element_type=jnp.float32
                )
                combined = combined + own_prob[rows] * own_values[token : token + 1]
                picked = combined[:, :HEAD_DIM]
                for g in range(1, groups):
                    columns = slice(g * HEAD_DIM, (g + 1) * HEAD_DIM)
                    picked = jnp.where(group_of == g, combined[:, columns], picked)
                mixed[token * heads : (token + 1) * heads, :] = picked
    for head in range(heads):
        columns = slice(head * HEAD_DIM, (head + 1) * HEAD_DIM)
        context_ref[:, columns] = mixed[pl.ds(head, row_count, stride=heads), :].astype(
            jnp.bfloat16
        )
    for copy in weights:
        copy.wait()


def attend_and_stage(held, cache_lengths, start, row_count, weights):
    width = held[0].shape[1]
    heads = width // HEAD_DIM
    vmem, hbm = pl.BlockSpec(memory_space=pltpu.VMEM), pl.BlockSpec(memory_space=pltpu.HBM)
    chunk = 8
    out = pl.pallas_call(
        functools.partial(attend_kernel, start=start, chunk=chunk, together=4),
        in_specs=[pl.BlockSpec(memory_space=pltpu.SMEM)] + [hbm] * (5 + len(weights)),
        out_specs=[vmem] * (1 + len(weights)),
        out_shape=[jax.ShapeDtypeStruct((row_count, width), held[0].dtype)]
        + [pltpu.VMEM(w.shape, w.dtype) for w in weights],
        scratch_shapes=[pltpu.VMEM((row_count,) + a.shape[1:], a.dtype) for a in held]
        + [pltpu.VMEM((row_count * heads, HEAD_DIM), jnp.float32)] * 2
        + [pltpu.SemaphoreType.DMA((4, max(4, -(-row_count // chunk))))],
        compiler_params=pltpu.CompilerParams(vmem_limit_bytes=10 * 1024 * 1024),
        cost_estimate=pl.CostEstimate(
            flops=4 * row_count * heads * held[1].shape[1] * held[1].shape[2],
            bytes_accessed=4 * row_count * held[1].shape[1] * held[1].shape[2]
            + sum(2 * w.size for w in weights),
            transcendentals=row_count * heads * held[1].shape[1],
        ),
        name="attend_and_stage",
    )(cache_lengths, *in_hbm(*held, *weights))
    return out[0], out[1:]


def stage_kernel(*refs):
    count = (len(refs) - 2) // 2
    refs[-2][...] = jnp.zeros(refs[-2].shape, jnp.float32)
    copies = [
        pltpu.make_async_copy(refs[j], refs[count + j], refs[-1].at[j]) for j in range(count)
    ]
    for copy in copies:
        copy.start()
    for copy in copies:
        copy.wait()


def staged(weights):
    return pl.pallas_call(
        stage_kernel,
        in_specs=[pl.BlockSpec(memory_space=pltpu.HBM)] * len(weights),
        out_specs=[pl.BlockSpec(memory_space=pltpu.VMEM)] * (len(weights) + 1),
        out_shape=[pltpu.VMEM(w.shape, w.dtype) for w in weights]
        + [jax.ShapeDtypeStruct((8, 128), jnp.float32)],
        scratch_shapes=[pltpu.SemaphoreType.DMA((len(weights),))],
        compiler_params=pltpu.CompilerParams(vmem_limit_bytes=4 * 1024 * 1024),
        cost_estimate=pl.CostEstimate(
            flops=0, bytes_accessed=sum(4 * w.size for w in weights), transcendentals=0
        ),
        name="stage_weights",
    )(*in_hbm(*weights))


def norm_kernel(side_ref, *refs):
    sources, (rows_ref, half_ref), held, sems = refs[:4], refs[4:6], refs[6:10], refs[10]
    copies = [
        pltpu.make_async_copy(source, target, sems.at[j])
        for j, (source, target) in enumerate(zip(sources, held))
    ]
    for copy in copies:
        copy.start()
    for copy in copies:
        copy.wait()
    hidden_ref, gain_ref, ids_ref, probs_ref = held
    features = hidden_ref.shape[1]
    row_count = hidden_ref.shape[0]
    lanes = rows_ref.shape[1] - features
    wide = hidden_ref[...].astype(jnp.float32)
    inverse = lax.rsqrt(jnp.mean(wide * wide, axis=1, keepdims=True) + 1e-06)
    normed = wide * inverse * gain_ref[...].astype(jnp.float32).reshape(1, features)
    probs = probs_ref[...]
    share = probs / jnp.sum(probs, axis=0, keepdims=True)
    ids = ids_ref[...]
    place = lax.broadcasted_iota(jnp.int32, (lanes, row_count), 0)
    half_lanes = lanes // 2
    expert_of = jnp.where(place < half_lanes, place, place - half_lanes)
    gates = jnp.zeros((lanes, row_count), jnp.float32)
    for k in range(ids.shape[0]):
        gates = gates + jnp.where(expert_of == ids[k : k + 1], share[k : k + 1], 0.0)
    coarse = gates.astype(jnp.bfloat16).astype(jnp.float32)
    gates = jnp.where(place < half_lanes, coarse, gates - coarse).T
    half = row_count // 2
    first = side_ref[0] == 0

    def store(columns, values):
        values = values.astype(jnp.bfloat16)
        mine = jnp.where(first, values[:half], values[half:])
        rows_ref[:half, columns] = mine
        rows_ref[half:, columns] = jnp.where(first, values[half:], values[:half])
        half_ref[:, columns] = mine

    store(slice(0, features), normed)
    store(slice(features, features + lanes), gates)


def normed_rows(hidden, norm_gain, expert_ids, router_probs, experts):
    row_count, features = hidden.shape
    lanes = 128 * (-(-2 * experts // 128))
    side = lax.axis_index("side").astype(jnp.int32).reshape(1)
    width = features + lanes
    vmem, hbm = pl.BlockSpec(memory_space=pltpu.VMEM), pl.BlockSpec(memory_space=pltpu.HBM)
    held = (hidden, norm_gain, expert_ids.T, router_probs.T)
    return pl.pallas_call(
        norm_kernel,
        in_specs=[pl.BlockSpec(memory_space=pltpu.SMEM)] + [hbm] * 4,
        out_specs=(vmem, vmem),
        out_shape=(
            jax.ShapeDtypeStruct((row_count, width), jnp.bfloat16),
            jax.ShapeDtypeStruct((row_count // 2, width), jnp.bfloat16),
        ),
        scratch_shapes=[pltpu.VMEM(a.shape, a.dtype) for a in held]
        + [pltpu.SemaphoreType.DMA((4,))],
        compiler_params=pltpu.CompilerParams(vmem_limit_bytes=8 * 1024 * 1024),
        name="norm_and_gates",
    )(side, *in_hbm(*held))


def expert_kernel(expert_ref, *refs):
    gate_ref, up_ref, down_ref, own_out, other_out, activation = refs[-6:]
    features = gate_ref.shape[1]
    rows = own_out.shape[0]
    x = jnp.concatenate([ref[:, :features] for ref in refs[:-6]], axis=0)
    tail = jnp.concatenate([ref[:, features:] for ref in refs[:-6]], axis=0)
    lanes = tail.shape[1]
    lane = lax.broadcasted_iota(jnp.int32, tail.shape, 1)
    mine = (lane == expert_ref[0]) | (lane == expert_ref[0] + lanes // 2)
    share = jnp.sum(jnp.where(mine, tail.astype(jnp.float32), 0.0), axis=1, keepdims=True)
    for low in range(0, gate_ref.shape[2], 256):
        units = slice(low, low + 256)
        gate_act = jnp.dot(x, gate_ref[0, :, units], preferred_element_type=jnp.float32)
        up_act = jnp.dot(x, up_ref[0, :, units], preferred_element_type=jnp.float32)
        activation[:, units] = (jax.nn.silu(gate_act) * up_act * share).astype(jnp.bfloat16)
    hidden_units = activation[...]
    for low in range(0, features, 1024):
        columns = slice(low, low + 1024)
        part = jnp.dot(
            hidden_units, down_ref[0, :, columns], preferred_element_type=jnp.float32
        ).astype(jnp.bfloat16)
        own_out[:, columns] = part[:rows]
        other_out[:, columns] = part[rows:]


def expert_rows(own, other, weights):
    rows = sum(a.shape[0] for a in own)
    _, features, hidden_units = weights[0].shape
    expert = lax.axis_index("dev").astype(jnp.int32).reshape(1)
    vmem = pl.BlockSpec(memory_space=pltpu.VMEM)
    return pl.pallas_call(
        expert_kernel,
        in_specs=[pl.BlockSpec(memory_space=pltpu.SMEM)] + [vmem] * (2 * len(own) + 3),
        out_specs=(vmem, vmem),
        out_shape=(jax.ShapeDtypeStruct((rows, features), jnp.bfloat16),) * 2,
        scratch_shapes=[pltpu.VMEM((2 * rows, hidden_units), jnp.bfloat16)],
        compiler_params=pltpu.CompilerParams(vmem_limit_bytes=16 * 1024 * 1024),
        cost_estimate=pl.CostEstimate(
            flops=12 * rows * features * hidden_units,
            bytes_accessed=6 * features * hidden_units,
            transcendentals=2 * rows * hidden_units,
        ),
        name="expert_rows",
    )(
        expert,
        *own,
        *other,
        *(pltpu.with_memory_space_constraint(w, pltpu.VMEM) for w in weights),
    )


def add(*parts):
    total = parts[0].astype(jnp.float32)
    for part in parts[1:]:
        total = total + part.astype(jnp.float32)
    return total


def add_rounded(*parts):
    return add(*parts).astype(jnp.bfloat16)


def per_device(
    queries,
    cache_keys,
    cache_values,
    new_key,
    new_value,
    cache_lengths,
    hidden,
    norm_gain,
    expert_ids,
    router_probs,
    w_gate,
    w_up,
    w_down,
):
    devices = lax.axis_size("dev")
    planes = devices // 4
    experts = w_gate.shape[0] * devices

    def over(bit):
        return lambda a: lax.ppermute(a, "dev", [(d, d ^ bit) for d in range(devices)])

    core, across = over(1), over(2)
    sides = lambda a: lax.ppermute(a, "side", [(0, 1), (1, 0)])

    def opposite(a):
        pairs = [
            (s * devices + d, (1 - s) * devices + (d ^ 2)) for s in range(2) for d in range(devices)
        ]
        return lax.ppermute(a, ("side", "dev"), pairs)

    own_rows, own_half = normed_rows(hidden, norm_gain, expert_ids, router_probs, experts)
    half = own_half.shape[0]
    arrived = {i: over(4 * i)(own_half) for i in range(1, planes) if i != 3}
    beside_own = across(own_rows)
    held = (queries, cache_keys, cache_values, new_key, new_value)
    part = queries.shape[0] // 2
    tie = lax.optimization_barrier

    first_context, _ = attend_and_stage(held, cache_lengths, 0, part, ())
    near, cache_lengths, first_context = tie((arrived[2], cache_lengths, first_context))
    arrived[3] = over(4)(near)
    near_rows = [near, opposite(near), across(near), sides(near)]

    far = {}
    pairs = [(0, 2), (1, 3)] + [(i, i + 1) for i in range(4, planes, 2)]
    for first, second in pairs[1:]:
        far[first] = jnp.concatenate([arrived[first], arrived[second]], axis=0)
    beside_own, far, w_gate = tie((beside_own, far, w_gate))
    far_beside = {first: across(rows) for first, rows in far.items()}
    far_facing = {first: sides(rows) for first, rows in far.items()}

    *weights, done = staged((w_gate, w_up, w_down))
    near_rows, far_beside, far_facing, done = tie((near_rows, far_beside, far_facing, done))

    stack = jnp.concatenate([own_rows, beside_own, *near_rows], axis=0)
    blocks = {0: ((stack,), (core(stack),))}
    for first, rows in far.items():
        beside, facing = far_beside[first], far_facing[first]
        late = jnp.concatenate([sides(beside[:half]), across(facing[half:])], axis=0)
        early = jnp.concatenate([rows, facing, beside], axis=0)
        blocks[first] = ((early, late), (core(early), core(late)))

    def by_plane(first, merged):
        rows = [merged[j * half : (j + 1) * half] for j in range(8)]
        if first == 0:
            return [rows[4], rows[7], rows[6], rows[5]], rows[:4]
        return rows[0::2], rows[1::2]

    def to_send(first, merged):
        one, two = by_plane(first, merged)
        return (
            jnp.concatenate([one[1], one[3]], axis=0),
            jnp.concatenate([two[2], two[3]], axis=0),
        )

    reduced = {}

    def exchange(sent):
        return sides(sent[0]), across(sent[1])

    def step(first, second, merged, got):
        one, two = by_plane(first, merged)
        by_side, by_row = (second, first) if first == 0 else (first, second)
        got_side, got_row = got
        return {
            by_side: (add(one[0], got_side[:half]), across(add_rounded(one[2], got_side[half:]))),
            by_row: (add(two[0], got_row[:half]), sides(add_rounded(two[1], got_row[half:]))),
        }

    def finish(parts):
        for i, pair in parts.items():
            reduced[i] = add(*pair) if i == 0 else over(4 * i)(add_rounded(*pair))

    waiting = parts = None
    for pair in pairs:
        first = pair[0]
        if waiting is not None:
            blocks[first], waiting = tie((blocks[first], waiting))
            got = exchange(waiting[1])
        own_out, other_out = expert_rows(*blocks[first], weights)
        if waiting is not None:
            own_out, other_out, got = tie((own_out, other_out, got))
            if parts is not None:
                finish(parts)
            parts = step(*before, waiting[0], got)
        merged = add_rounded(own_out, core(other_out))
        waiting, before = (merged, to_send(first, merged)), pair
    waiting, cache_lengths = tie((waiting, cache_lengths))
    second_context, _ = attend_and_stage(
        held, cache_lengths, part, queries.shape[0] - part, ()
    )
    context = jnp.concatenate([first_context, second_context], axis=0)
    got, parts = tie((exchange(waiting[1]), parts))
    finish(parts)
    parts = step(*before, waiting[0], got)
    parts, reduced = tie((parts, reduced))
    finish(parts)
    total = add_rounded(*(reduced[i] for i in range(planes)))
    partner = sides(total)
    first = lax.axis_index("side") == 0
    moe_out = jnp.concatenate(
        [jnp.where(first, total, partner), jnp.where(first, partner, total)], axis=0
    )
    return (context, moe_out)


def solution(mesh):
    in_specs = (
        P("dev", "side"),
        P("dev", None, "side"),
        P("dev", None, "side"),
        P("dev", "side"),
        P("dev", "side"),
        P("dev"),
        P("dev", None),
        P(),
        P("dev", None),
        P("dev", None),
        P("dev", None, "side"),
        P("dev", None, "side"),
        P("dev", "side", None),
    )
    out_specs = (P("dev", "side"), P("dev", None))
    return jax.shard_map(
        per_device, mesh=mesh, in_specs=in_specs, out_specs=out_specs, check_vma=False
    )
```

```python
import functools

import jax
import jax.numpy as jnp
from jax import lax
from jax.experimental import pallas as pl
from jax.experimental.pallas import tpu as pltpu
from jax.sharding import PartitionSpec as P

HEADS = 64
KV_HEADS = 4
HEAD_DIM = 128


def in_hbm(*arrays):
    return [pltpu.with_memory_space_constraint(a, pltpu.HBM) for a in arrays]


def attend_kernel(
    lengths_ref,
    query_src,
    key_src,
    value_src,
    new_key_src,
    new_value_src,
    *rest,
    start,
    chunk,
    together,
):
    staged = (len(rest) - 9) // 2
    weight_srcs, context_ref, weight_refs = (
        rest[:staged],
        rest[staged],
        rest[staged + 1 : 2 * staged + 1],
    )
    queries, keys, values, new_key, new_value, by_token, mixed, sems = rest[2 * staged + 1 :]
    row_count, cache_len, width = keys.shape
    groups = width // HEAD_DIM
    per_group = HEADS // KV_HEADS
    heads = groups * per_group
    score_scale = HEAD_DIM ** (-0.5)
    small = [
        pltpu.make_async_copy(source.at[pl.ds(start, row_count)], target, sems.at[0, j])
        for j, (source, target) in enumerate(
            ((query_src, queries), (new_key_src, new_key), (new_value_src, new_value))
        )
    ]
    cached = [
        [
            pltpu.make_async_copy(
                source.at[pl.ds(start + low, chunk)],
                target.at[pl.ds(low, chunk)],
                sems.at[1 + j, place],
            )
            for j, (source, target) in enumerate(((key_src, keys), (value_src, values)))
        ]
        for place, low in enumerate(range(0, row_count, chunk))
    ]
    weights = [
        pltpu.make_async_copy(source, target, sems.at[3, j])
        for j, (source, target) in enumerate(zip(weight_srcs, weight_refs))
    ]
    for copy in small + sum(cached, []) + weights:
        copy.start()
    for copy in small:
        copy.wait()
    for head in range(heads):
        columns = slice(head * HEAD_DIM, (head + 1) * HEAD_DIM)
        by_token[pl.ds(head, row_count, stride=heads), :] = queries[:, columns].astype(jnp.float32)
    group_of = lax.broadcasted_iota(jnp.int32, (heads, HEAD_DIM), 0) // per_group
    position = lax.broadcasted_iota(jnp.int32, (heads, cache_len), 1)
    own_keys = new_key[...].astype(jnp.float32)
    own_values = new_value[...].astype(jnp.float32)
    for place, low in enumerate(range(0, row_count, chunk)):
        for copy in cached[place]:
            copy.wait()
        for first in range(low, low + chunk, together):
            tokens = range(first, first + together)
            spread, scores, own_score = [], [], []
            for token in tokens:
                query = by_token[token * heads : (token + 1) * heads, :]
                spread = jnp.concatenate(
                    [jnp.where(group_of == g, query, 0.0) for g in range(groups)], axis=1
                )
                score = lax.dot_general(
                    spread.astype(jnp.bfloat16),
                    keys[token],
                    (((1,), (1,)), ((), ())),
                    preferred_element_type=jnp.float32,
                )
                scores.append(
                    jnp.where(position < lengths_ref[start + token], score * score_scale, -1e30)
                )
                own_score.append(
                    jnp.sum(spread * own_keys[token : token + 1], axis=1, keepdims=True)
                )
            scores = jnp.concatenate(scores, axis=0)
            own_score = jnp.concatenate(own_score, axis=0) * score_scale
            top_score = jnp.maximum(jnp.max(scores, axis=1, keepdims=True), own_score)
            exp_scores = jnp.exp(scores - top_score)
            own_exp = jnp.exp(own_score - top_score)
            inverse = 1.0 / (jnp.sum(exp_scores, axis=1, keepdims=True) + own_exp)
            attn_weights = (exp_scores * inverse).astype(jnp.bfloat16)
            own_prob = (own_exp * inverse).astype(jnp.bfloat16).astype(jnp.float32)
            for place_of, token in enumerate(tokens):
                rows = slice(place_of * heads, (place_of + 1) * heads)
                combined = jnp.dot(
                    attn_weights[rows], values[token], preferred_element_type=jnp.float32
                )
                combined = combined + own_prob[rows] * own_values[token : token + 1]
                picked = combined[:, :HEAD_DIM]
                for g in range(1, groups):
                    columns = slice(g * HEAD_DIM, (g + 1) * HEAD_DIM)
                    picked = jnp.where(group_of == g, combined[:, columns], picked)
                mixed[token * heads : (token + 1) * heads, :] = picked
    for head in range(heads):
        columns = slice(head * HEAD_DIM, (head + 1) * HEAD_DIM)
        context_ref[:, columns] = mixed[pl.ds(head, row_count, stride=heads), :].astype(
            jnp.bfloat16
        )
    for copy in weights:
        copy.wait()


def attend_and_stage(held, cache_lengths, start, row_count, weights):
    width = held[0].shape[1]
    heads = width // HEAD_DIM
    vmem, hbm = pl.BlockSpec(memory_space=pltpu.VMEM), pl.BlockSpec(memory_space=pltpu.HBM)
    chunk = 8
    out = pl.pallas_call(
        functools.partial(attend_kernel, start=start, chunk=chunk, together=8),
        in_specs=[pl.BlockSpec(memory_space=pltpu.SMEM)] + [hbm] * (5 + len(weights)),
        out_specs=[vmem] * (1 + len(weights)),
        out_shape=[jax.ShapeDtypeStruct((row_count, width), held[0].dtype)]
        + [pltpu.VMEM(w.shape, w.dtype) for w in weights],
        scratch_shapes=[pltpu.VMEM((row_count,) + a.shape[1:], a.dtype) for a in held]
        + [pltpu.VMEM((row_count * heads, HEAD_DIM), jnp.float32)] * 2
        + [pltpu.SemaphoreType.DMA((4, max(4, -(-row_count // chunk))))],
        compiler_params=pltpu.CompilerParams(vmem_limit_bytes=10 * 1024 * 1024),
        cost_estimate=pl.CostEstimate(
            flops=4 * row_count * heads * held[1].shape[1] * held[1].shape[2],
            bytes_accessed=4 * row_count * held[1].shape[1] * held[1].shape[2]
            + sum(2 * w.size for w in weights),
            transcendentals=row_count * heads * held[1].shape[1],
        ),
        name="attend_and_stage",
    )(cache_lengths, *in_hbm(*held, *weights))
    return out[0], out[1:]


def stage_kernel(*refs):
    count = (len(refs) - 2) // 2
    refs[-2][...] = jnp.zeros(refs[-2].shape, jnp.float32)
    copies = [
        pltpu.make_async_copy(refs[j], refs[count + j], refs[-1].at[j]) for j in range(count)
    ]
    for copy in copies:
        copy.start()
    for copy in copies:
        copy.wait()


def staged(weights):
    return pl.pallas_call(
        stage_kernel,
        in_specs=[pl.BlockSpec(memory_space=pltpu.HBM)] * len(weights),
        out_specs=[pl.BlockSpec(memory_space=pltpu.VMEM)] * (len(weights) + 1),
        out_shape=[pltpu.VMEM(w.shape, w.dtype) for w in weights]
        + [jax.ShapeDtypeStruct((8, 128), jnp.float32)],
        scratch_shapes=[pltpu.SemaphoreType.DMA((len(weights),))],
        compiler_params=pltpu.CompilerParams(vmem_limit_bytes=4 * 1024 * 1024),
        cost_estimate=pl.CostEstimate(
            flops=0, bytes_accessed=sum(4 * w.size for w in weights), transcendentals=0
        ),
        name="stage_weights",
    )(*in_hbm(*weights))


def norm_kernel(side_ref, *refs):
    sources, (rows_ref, half_ref), held, sems = refs[:4], refs[4:6], refs[6:10], refs[10]
    copies = [
        pltpu.make_async_copy(source, target, sems.at[j])
        for j, (source, target) in enumerate(zip(sources, held))
    ]
    for copy in copies:
        copy.start()
    for copy in copies:
        copy.wait()
    hidden_ref, gain_ref, ids_ref, probs_ref = held
    features = hidden_ref.shape[1]
    row_count = hidden_ref.shape[0]
    lanes = rows_ref.shape[1] - features
    wide = hidden_ref[...].astype(jnp.float32)
    inverse = lax.rsqrt(jnp.mean(wide * wide, axis=1, keepdims=True) + 1e-06)
    normed = wide * inverse * gain_ref[...].astype(jnp.float32).reshape(1, features)
    probs = probs_ref[...]
    share = probs / jnp.sum(probs, axis=0, keepdims=True)
    ids = ids_ref[...]
    place = lax.broadcasted_iota(jnp.int32, (lanes, row_count), 0)
    half_lanes = lanes // 2
    expert_of = jnp.where(place < half_lanes, place, place - half_lanes)
    gates = jnp.zeros((lanes, row_count), jnp.float32)
    for k in range(ids.shape[0]):
        gates = gates + jnp.where(expert_of == ids[k : k + 1], share[k : k + 1], 0.0)
    coarse = gates.astype(jnp.bfloat16).astype(jnp.float32)
    gates = jnp.where(place < half_lanes, coarse, gates - coarse).T
    half = row_count // 2
    first = side_ref[0] == 0

    def store(columns, values):
        values = values.astype(jnp.bfloat16)
        mine = jnp.where(first, values[:half], values[half:])
        rows_ref[:half, columns] = mine
        rows_ref[half:, columns] = jnp.where(first, values[half:], values[:half])
        half_ref[:, columns] = mine

    store(slice(0, features), normed)
    store(slice(features, features + lanes), gates)


def normed_rows(hidden, norm_gain, expert_ids, router_probs, experts):
    row_count, features = hidden.shape
    lanes = 128 * (-(-2 * experts // 128))
    side = lax.axis_index("side").astype(jnp.int32).reshape(1)
    width = features + lanes
    vmem, hbm = pl.BlockSpec(memory_space=pltpu.VMEM), pl.BlockSpec(memory_space=pltpu.HBM)
    held = (hidden, norm_gain, expert_ids.T, router_probs.T)
    return pl.pallas_call(
        norm_kernel,
        in_specs=[pl.BlockSpec(memory_space=pltpu.SMEM)] + [hbm] * 4,
        out_specs=(vmem, vmem),
        out_shape=(
            jax.ShapeDtypeStruct((row_count, width), jnp.bfloat16),
            jax.ShapeDtypeStruct((row_count // 2, width), jnp.bfloat16),
        ),
        scratch_shapes=[pltpu.VMEM(a.shape, a.dtype) for a in held]
        + [pltpu.SemaphoreType.DMA((4,))],
        compiler_params=pltpu.CompilerParams(vmem_limit_bytes=8 * 1024 * 1024),
        name="norm_and_gates",
    )(side, *in_hbm(*held))


def expert_kernel(expert_ref, *refs):
    gate_ref, up_ref, down_ref, own_out, other_out, activation = refs[-6:]
    features = gate_ref.shape[1]
    rows = own_out.shape[0]
    x = jnp.concatenate([ref[:, :features] for ref in refs[:-6]], axis=0)
    tail = jnp.concatenate([ref[:, features:] for ref in refs[:-6]], axis=0)
    lanes = tail.shape[1]
    lane = lax.broadcasted_iota(jnp.int32, tail.shape, 1)
    mine = (lane == expert_ref[0]) | (lane == expert_ref[0] + lanes // 2)
    share = jnp.sum(jnp.where(mine, tail.astype(jnp.float32), 0.0), axis=1, keepdims=True)
    for low in range(0, gate_ref.shape[2], 256):
        units = slice(low, low + 256)
        gate_act = jnp.dot(x, gate_ref[0, :, units], preferred_element_type=jnp.float32)
        up_act = jnp.dot(x, up_ref[0, :, units], preferred_element_type=jnp.float32)
        activation[:, units] = (jax.nn.silu(gate_act) * up_act * share).astype(jnp.bfloat16)
    hidden_units = activation[...]
    for low in range(0, features, 1024):
        columns = slice(low, low + 1024)
        part = jnp.dot(
            hidden_units, down_ref[0, :, columns], preferred_element_type=jnp.float32
        ).astype(jnp.bfloat16)
        own_out[:, columns] = part[:rows]
        other_out[:, columns] = part[rows:]


def expert_rows(own, other, weights):
    rows = own.shape[0]
    _, features, hidden_units = weights[0].shape
    expert = lax.axis_index("dev").astype(jnp.int32).reshape(1)
    vmem = pl.BlockSpec(memory_space=pltpu.VMEM)
    return pl.pallas_call(
        expert_kernel,
        in_specs=[pl.BlockSpec(memory_space=pltpu.SMEM)] + [vmem] * 5,
        out_specs=(vmem, vmem),
        out_shape=(jax.ShapeDtypeStruct((rows, features), jnp.bfloat16),) * 2,
        scratch_shapes=[pltpu.VMEM((2 * rows, hidden_units), jnp.bfloat16)],
        compiler_params=pltpu.CompilerParams(vmem_limit_bytes=16 * 1024 * 1024),
        cost_estimate=pl.CostEstimate(
            flops=12 * rows * features * hidden_units,
            bytes_accessed=6 * features * hidden_units,
            transcendentals=2 * rows * hidden_units,
        ),
        name="expert_rows",
    )(
        expert,
        own,
        other,
        *(pltpu.with_memory_space_constraint(w, pltpu.VMEM) for w in weights),
    )


def add(*parts):
    total = parts[0].astype(jnp.float32)
    for part in parts[1:]:
        total = total + part.astype(jnp.float32)
    return total


def add_rounded(*parts):
    return add(*parts).astype(jnp.bfloat16)


def per_device(
    queries,
    cache_keys,
    cache_values,
    new_key,
    new_value,
    cache_lengths,
    hidden,
    norm_gain,
    expert_ids,
    router_probs,
    w_gate,
    w_up,
    w_down,
):
    devices = lax.axis_size("dev")
    planes = devices // 4
    experts = w_gate.shape[0] * devices

    def over(bit):
        return lambda a: lax.ppermute(a, "dev", [(d, d ^ bit) for d in range(devices)])

    core, across = over(1), over(2)
    sides = lambda a: lax.ppermute(a, "side", [(0, 1), (1, 0)])

    def opposite(a):
        pairs = [
            (s * devices + d, (1 - s) * devices + (d ^ 2)) for s in range(2) for d in range(devices)
        ]
        return lax.ppermute(a, ("side", "dev"), pairs)

    own_rows, own_half = normed_rows(hidden, norm_gain, expert_ids, router_probs, experts)
    half = own_half.shape[0]
    tie = lax.optimization_barrier
    held = (queries, cache_keys, cache_values, new_key, new_value)
    part = queries.shape[0] // 2
    direct = [i for i in range(1, planes) if i not in (2, 3)]
    pairs = [(i, i + 2) for i in range(planes) if i % 4 < 2]

    second_half = over(8)(own_half)
    own_of = {i: over(4 * i)(own_rows) for i in direct}
    own_of[0], beside_of = own_rows, {0: across(own_rows)}
    *weights, done = staged((w_gate, w_up, w_down))
    second_half, beside_of[0], done = tie((second_half, beside_of[0], done))
    third_half = over(4)(second_half)

    around = [sides(second_half), across(second_half), opposite(second_half)]
    for i in direct:
        beside_of[i] = over(4 * i)(beside_of[0])
    around = jnp.concatenate(around, axis=0)
    blocks = {i: [own_of[i], beside_of[i]] for i in [0] + direct}
    blocks[2] = [second_half, around]
    blocks[3] = [third_half, over(4)(around)]
    stacks = {}
    for first, second in pairs:
        stack = jnp.concatenate(blocks[first] + blocks[second], axis=0)
        stacks[first] = (stack, core(stack))

    def by_plane(merged):
        rows = [merged[j * half : (j + 1) * half] for j in range(8)]
        return rows[4:], rows[:4]

    def to_send(merged):
        one, two = by_plane(merged)
        return (
            jnp.concatenate([one[1], one[3]], axis=0),
            jnp.concatenate([two[2], two[3]], axis=0),
        )

    reduced = {}

    def exchange(sent):
        return sides(sent[0]), across(sent[1])

    def step(first, second, merged, got):
        one, two = by_plane(merged)
        by_side, by_row = second, first
        got_side, got_row = got
        return {
            by_side: (add(one[0], got_side[:half]), across(add_rounded(one[2], got_side[half:]))),
            by_row: (add(two[0], got_row[:half]), sides(add_rounded(two[1], got_row[half:]))),
        }

    def finish(parts):
        for i, pair in parts.items():
            reduced[i] = add(*pair) if i == 0 else over(4 * i)(add_rounded(*pair))

    waiting = parts = None
    for pair in pairs:
        first = pair[0]
        if waiting is not None:
            stacks[first], waiting = tie((stacks[first], waiting))
            got = exchange(waiting[1])
        own_out, other_out = expert_rows(*stacks[first], weights)
        if waiting is not None:
            own_out, other_out, got = tie((own_out, other_out, got))
            if parts is not None:
                finish(parts)
            parts = step(*before, waiting[0], got)
        merged = add_rounded(own_out, core(other_out))
        waiting, before = (merged, to_send(merged)), pair
    waiting, cache_lengths = tie((waiting, cache_lengths))
    got = exchange(waiting[1])
    first_context, _ = attend_and_stage(held, cache_lengths, 0, part, ())
    got, parts, first_context, cache_lengths = tie((got, parts, first_context, cache_lengths))
    finish(parts)
    parts = step(*before, waiting[0], got)
    parts, reduced, cache_lengths = tie((parts, reduced, cache_lengths))
    finish(parts)
    second_context, _ = attend_and_stage(
        held, cache_lengths, part, queries.shape[0] - part, ()
    )
    context = jnp.concatenate([first_context, second_context], axis=0)
    total = add_rounded(*(reduced[i] for i in range(planes)))
    partner = sides(total)
    first = lax.axis_index("side") == 0
    moe_out = jnp.concatenate(
        [jnp.where(first, total, partner), jnp.where(first, partner, total)], axis=0
    )
    return (context, moe_out)


def solution(mesh):
    in_specs = (
        P("dev", "side"),
        P("dev", None, "side"),
        P("dev", None, "side"),
        P("dev", "side"),
        P("dev", "side"),
        P("dev"),
        P("dev", None),
        P(),
        P("dev", None),
        P("dev", None),
        P("dev", None, "side"),
        P("dev", None, "side"),
        P("dev", "side", None),
    )
    out_specs = (P("dev", "side"), P("dev", None))
    return jax.shard_map(
        per_device, mesh=mesh, in_specs=in_specs, out_specs=out_specs, check_vma=False
    )
```

```python
import functools

import jax
import jax.numpy as jnp
from jax import lax
from jax.experimental import pallas as pl
from jax.experimental.pallas import tpu as pltpu
from jax.sharding import PartitionSpec as P

HEADS = 64
KV_HEADS = 4
HEAD_DIM = 128


def in_hbm(*arrays):
    return [pltpu.with_memory_space_constraint(a, pltpu.HBM) for a in arrays]


def attend_kernel(
    lengths_ref,
    query_src,
    key_src,
    value_src,
    new_key_src,
    new_value_src,
    *rest,
    start,
    chunk,
    together,
):
    staged = (len(rest) - 9) // 2
    weight_srcs, context_ref, weight_refs = (
        rest[:staged],
        rest[staged],
        rest[staged + 1 : 2 * staged + 1],
    )
    queries, keys, values, new_key, new_value, by_token, mixed, sems = rest[2 * staged + 1 :]
    row_count, cache_len, width = keys.shape
    groups = width // HEAD_DIM
    per_group = HEADS // KV_HEADS
    heads = groups * per_group
    score_scale = HEAD_DIM ** (-0.5)
    small = [
        pltpu.make_async_copy(source.at[pl.ds(start, row_count)], target, sems.at[0, j])
        for j, (source, target) in enumerate(
            ((query_src, queries), (new_key_src, new_key), (new_value_src, new_value))
        )
    ]
    cached = [
        [
            pltpu.make_async_copy(
                source.at[pl.ds(start + low, chunk)],
                target.at[pl.ds(low, chunk)],
                sems.at[1 + j, place],
            )
            for j, (source, target) in enumerate(((key_src, keys), (value_src, values)))
        ]
        for place, low in enumerate(range(0, row_count, chunk))
    ]
    weights = [
        pltpu.make_async_copy(source, target, sems.at[3, j])
        for j, (source, target) in enumerate(zip(weight_srcs, weight_refs))
    ]
    for copy in small + sum(cached, []) + weights:
        copy.start()
    for copy in small:
        copy.wait()
    for head in range(heads):
        columns = slice(head * HEAD_DIM, (head + 1) * HEAD_DIM)
        by_token[pl.ds(head, row_count, stride=heads), :] = queries[:, columns].astype(jnp.float32)
    group_of = lax.broadcasted_iota(jnp.int32, (heads, HEAD_DIM), 0) // per_group
    position = lax.broadcasted_iota(jnp.int32, (heads, cache_len), 1)
    own_keys = new_key[...].astype(jnp.float32)
    own_values = new_value[...].astype(jnp.float32)
    for place, low in enumerate(range(0, row_count, chunk)):
        for copy in cached[place]:
            copy.wait()
        for first in range(low, low + chunk, together):
            tokens = range(first, first + together)
            spread, scores, own_score = [], [], []
            for token in tokens:
                query = by_token[token * heads : (token + 1) * heads, :]
                spread = jnp.concatenate(
                    [jnp.where(group_of == g, query, 0.0) for g in range(groups)], axis=1
                )
                score = lax.dot_general(
                    spread.astype(jnp.bfloat16),
                    keys[token],
                    (((1,), (1,)), ((), ())),
                    preferred_element_type=jnp.float32,
                )
                scores.append(
                    jnp.where(position < lengths_ref[start + token], score * score_scale, -1e30)
                )
                own_score.append(
                    jnp.sum(spread * own_keys[token : token + 1], axis=1, keepdims=True)
                )
            scores = jnp.concatenate(scores, axis=0)
            own_score = jnp.concatenate(own_score, axis=0) * score_scale
            top_score = jnp.maximum(jnp.max(scores, axis=1, keepdims=True), own_score)
            exp_scores = jnp.exp(scores - top_score)
            own_exp = jnp.exp(own_score - top_score)
            inverse = 1.0 / (jnp.sum(exp_scores, axis=1, keepdims=True) + own_exp)
            attn_weights = (exp_scores * inverse).astype(jnp.bfloat16)
            own_prob = (own_exp * inverse).astype(jnp.bfloat16).astype(jnp.float32)
            for place_of, token in enumerate(tokens):
                rows = slice(place_of * heads, (place_of + 1) * heads)
                combined = jnp.dot(
                    attn_weights[rows], values[token], preferred_element_type=jnp.float32
                )
                combined = combined + own_prob[rows] * own_values[token : token + 1]
                picked = combined[:, :HEAD_DIM]
                for g in range(1, groups):
                    columns = slice(g * HEAD_DIM, (g + 1) * HEAD_DIM)
                    picked = jnp.where(group_of == g, combined[:, columns], picked)
                mixed[token * heads : (token + 1) * heads, :] = picked
    for head in range(heads):
        columns = slice(head * HEAD_DIM, (head + 1) * HEAD_DIM)
        context_ref[:, columns] = mixed[pl.ds(head, row_count, stride=heads), :].astype(
            jnp.bfloat16
        )
    for copy in weights:
        copy.wait()


def attend_and_stage(held, cache_lengths, start, row_count, weights):
    width = held[0].shape[1]
    heads = width // HEAD_DIM
    vmem, hbm = pl.BlockSpec(memory_space=pltpu.VMEM), pl.BlockSpec(memory_space=pltpu.HBM)
    chunk = 8
    out = pl.pallas_call(
        functools.partial(attend_kernel, start=start, chunk=chunk, together=8),
        in_specs=[pl.BlockSpec(memory_space=pltpu.SMEM)] + [hbm] * (5 + len(weights)),
        out_specs=[vmem] * (1 + len(weights)),
        out_shape=[jax.ShapeDtypeStruct((row_count, width), held[0].dtype)]
        + [pltpu.VMEM(w.shape, w.dtype) for w in weights],
        scratch_shapes=[pltpu.VMEM((row_count,) + a.shape[1:], a.dtype) for a in held]
        + [pltpu.VMEM(((row_count + 1) * heads, HEAD_DIM), jnp.float32)] * 2
        + [pltpu.SemaphoreType.DMA((4, max(4, -(-row_count // chunk))))],
        compiler_params=pltpu.CompilerParams(vmem_limit_bytes=10 * 1024 * 1024),
        cost_estimate=pl.CostEstimate(
            flops=4 * row_count * heads * held[1].shape[1] * held[1].shape[2],
            bytes_accessed=4 * row_count * held[1].shape[1] * held[1].shape[2]
            + sum(2 * w.size for w in weights),
            transcendentals=row_count * heads * held[1].shape[1],
        ),
        name="attend_and_stage",
    )(cache_lengths, *in_hbm(*held, *weights))
    return out[0], out[1:]


def stage_kernel(*refs):
    count = (len(refs) - 2) // 2
    refs[-2][...] = jnp.zeros(refs[-2].shape, jnp.float32)
    copies = [
        pltpu.make_async_copy(refs[j], refs[count + j], refs[-1].at[j]) for j in range(count)
    ]
    for copy in copies:
        copy.start()
    for copy in copies:
        copy.wait()


def staged(weights):
    return pl.pallas_call(
        stage_kernel,
        in_specs=[pl.BlockSpec(memory_space=pltpu.HBM)] * len(weights),
        out_specs=[pl.BlockSpec(memory_space=pltpu.VMEM)] * (len(weights) + 1),
        out_shape=[pltpu.VMEM(w.shape, w.dtype) for w in weights]
        + [jax.ShapeDtypeStruct((8, 128), jnp.float32)],
        scratch_shapes=[pltpu.SemaphoreType.DMA((len(weights),))],
        compiler_params=pltpu.CompilerParams(vmem_limit_bytes=4 * 1024 * 1024),
        cost_estimate=pl.CostEstimate(
            flops=0, bytes_accessed=sum(4 * w.size for w in weights), transcendentals=0
        ),
        name="stage_weights",
    )(*in_hbm(*weights))


def norm_kernel(side_ref, *refs):
    sources, (rows_ref, half_ref), held, sems = refs[:4], refs[4:6], refs[6:10], refs[10]
    copies = [
        pltpu.make_async_copy(source, target, sems.at[j])
        for j, (source, target) in enumerate(zip(sources, held))
    ]
    for copy in copies:
        copy.start()
    for copy in copies:
        copy.wait()
    hidden_ref, gain_ref, ids_ref, probs_ref = held
    features = hidden_ref.shape[1]
    row_count = hidden_ref.shape[0]
    lanes = rows_ref.shape[1] - features
    wide = hidden_ref[...].astype(jnp.float32)
    inverse = lax.rsqrt(jnp.mean(wide * wide, axis=1, keepdims=True) + 1e-06)
    normed = wide * inverse * gain_ref[...].astype(jnp.float32).reshape(1, features)
    probs = probs_ref[...]
    share = probs / jnp.sum(probs, axis=0, keepdims=True)
    ids = ids_ref[...]
    place = lax.broadcasted_iota(jnp.int32, (lanes, row_count), 0)
    half_lanes = lanes // 2
    expert_of = jnp.where(place < half_lanes, place, place - half_lanes)
    gates = jnp.zeros((lanes, row_count), jnp.float32)
    for k in range(ids.shape[0]):
        gates = gates + jnp.where(expert_of == ids[k : k + 1], share[k : k + 1], 0.0)
    coarse = gates.astype(jnp.bfloat16).astype(jnp.float32)
    gates = jnp.where(place < half_lanes, coarse, gates - coarse).T
    half = row_count // 2
    first = side_ref[0] == 0

    def store(columns, values):
        values = values.astype(jnp.bfloat16)
        mine = jnp.where(first, values[:half], values[half:])
        rows_ref[:half, columns] = mine
        rows_ref[half:, columns] = jnp.where(first, values[half:], values[:half])
        half_ref[:, columns] = mine

    store(slice(0, features), normed)
    store(slice(features, features + lanes), gates)


def normed_rows(hidden, norm_gain, expert_ids, router_probs, experts):
    row_count, features = hidden.shape
    lanes = 128 * (-(-2 * experts // 128))
    side = lax.axis_index("side").astype(jnp.int32).reshape(1)
    width = features + lanes
    vmem, hbm = pl.BlockSpec(memory_space=pltpu.VMEM), pl.BlockSpec(memory_space=pltpu.HBM)
    held = (hidden, norm_gain, expert_ids.T, router_probs.T)
    return pl.pallas_call(
        norm_kernel,
        in_specs=[pl.BlockSpec(memory_space=pltpu.SMEM)] + [hbm] * 4,
        out_specs=(vmem, vmem),
        out_shape=(
            jax.ShapeDtypeStruct((row_count, width), jnp.bfloat16),
            jax.ShapeDtypeStruct((row_count // 2, width), jnp.bfloat16),
        ),
        scratch_shapes=[pltpu.VMEM(a.shape, a.dtype) for a in held]
        + [pltpu.SemaphoreType.DMA((4,))],
        compiler_params=pltpu.CompilerParams(vmem_limit_bytes=8 * 1024 * 1024),
        name="norm_and_gates",
    )(side, *in_hbm(*held))


def expert_kernel(expert_ref, *refs):
    gate_ref, up_ref, down_ref, own_out, other_out, activation = refs[-6:]
    features = gate_ref.shape[1]
    rows = own_out.shape[0]
    x = jnp.concatenate([ref[:, :features] for ref in refs[:-6]], axis=0)
    tail = jnp.concatenate([ref[:, features:] for ref in refs[:-6]], axis=0)
    lanes = tail.shape[1]
    lane = lax.broadcasted_iota(jnp.int32, tail.shape, 1)
    mine = (lane == expert_ref[0]) | (lane == expert_ref[0] + lanes // 2)
    share = jnp.sum(jnp.where(mine, tail.astype(jnp.float32), 0.0), axis=1, keepdims=True)
    for low in range(0, gate_ref.shape[2], 256):
        units = slice(low, low + 256)
        gate_act = jnp.dot(x, gate_ref[0, :, units], preferred_element_type=jnp.float32)
        up_act = jnp.dot(x, up_ref[0, :, units], preferred_element_type=jnp.float32)
        activation[:, units] = (jax.nn.silu(gate_act) * up_act * share).astype(jnp.bfloat16)
    hidden_units = activation[...]
    for low in range(0, features, 1024):
        columns = slice(low, low + 1024)
        part = jnp.dot(
            hidden_units, down_ref[0, :, columns], preferred_element_type=jnp.float32
        ).astype(jnp.bfloat16)
        own_out[:, columns] = part[:rows]
        other_out[:, columns] = part[rows:]


def expert_rows(own, other, weights):
    rows = own.shape[0]
    _, features, hidden_units = weights[0].shape
    expert = lax.axis_index("dev").astype(jnp.int32).reshape(1)
    vmem = pl.BlockSpec(memory_space=pltpu.VMEM)
    return pl.pallas_call(
        expert_kernel,
        in_specs=[pl.BlockSpec(memory_space=pltpu.SMEM)] + [vmem] * 5,
        out_specs=(vmem, vmem),
        out_shape=(jax.ShapeDtypeStruct((rows, features), jnp.bfloat16),) * 2,
        scratch_shapes=[pltpu.VMEM((2 * rows, hidden_units), jnp.bfloat16)],
        compiler_params=pltpu.CompilerParams(vmem_limit_bytes=16 * 1024 * 1024),
        cost_estimate=pl.CostEstimate(
            flops=12 * rows * features * hidden_units,
            bytes_accessed=6 * features * hidden_units,
            transcendentals=2 * rows * hidden_units,
        ),
        name="expert_rows",
    )(
        expert,
        own,
        other,
        *(pltpu.with_memory_space_constraint(w, pltpu.VMEM) for w in weights),
    )


def add(*parts):
    total = parts[0].astype(jnp.float32)
    for part in parts[1:]:
        total = total + part.astype(jnp.float32)
    return total


def add_rounded(*parts):
    return add(*parts).astype(jnp.bfloat16)


def per_device(
    queries,
    cache_keys,
    cache_values,
    new_key,
    new_value,
    cache_lengths,
    hidden,
    norm_gain,
    expert_ids,
    router_probs,
    w_gate,
    w_up,
    w_down,
):
    devices = lax.axis_size("dev")
    planes = devices // 4
    experts = w_gate.shape[0] * devices

    def over(bit):
        return lambda a: lax.ppermute(a, "dev", [(d, d ^ bit) for d in range(devices)])

    core, across = over(1), over(2)
    sides = lambda a: lax.ppermute(a, "side", [(0, 1), (1, 0)])

    def opposite(a):
        pairs = [
            (s * devices + d, (1 - s) * devices + (d ^ 2)) for s in range(2) for d in range(devices)
        ]
        return lax.ppermute(a, ("side", "dev"), pairs)

    own_rows, own_half = normed_rows(hidden, norm_gain, expert_ids, router_probs, experts)
    half = own_half.shape[0]
    tie = lax.optimization_barrier
    held = (queries, cache_keys, cache_values, new_key, new_value)
    part = queries.shape[0] // 2
    direct = [i for i in range(1, planes) if i not in (2, 3)]
    pairs = [(i, i + 2) for i in range(planes) if i % 4 < 2]

    second_half = over(8)(own_half)
    own_of = {i: over(4 * i)(own_rows) for i in direct}
    own_of[0], beside_of = own_rows, {0: across(own_rows)}
    *weights, done = staged((w_gate, w_up, w_down))
    second_half, beside_of[0], done = tie((second_half, beside_of[0], done))
    third_half = over(4)(second_half)

    around = [sides(second_half), across(second_half), opposite(second_half)]
    for i in direct:
        beside_of[i] = over(4 * i)(beside_of[0])
    around = jnp.concatenate(around, axis=0)
    blocks = {i: [own_of[i], beside_of[i]] for i in [0] + direct}
    blocks[2] = [second_half, around]
    blocks[3] = [third_half, over(4)(around)]
    stacks = {}
    for first, second in pairs:
        stack = jnp.concatenate(blocks[first] + blocks[second], axis=0)
        stacks[first] = (stack, core(stack))

    def by_plane(merged):
        rows = [merged[j * half : (j + 1) * half] for j in range(8)]
        return rows[4:], rows[:4]

    def to_send(merged):
        one, two = by_plane(merged)
        return (
            jnp.concatenate([one[1], one[3]], axis=0),
            jnp.concatenate([two[2], two[3]], axis=0),
        )

    reduced = {}

    def exchange(sent):
        return sides(sent[0]), across(sent[1])

    def step(first, second, merged, got):
        one, two = by_plane(merged)
        by_side, by_row = second, first
        got_side, got_row = got
        return {
            by_side: (add(one[0], got_side[:half]), across(add_rounded(one[2], got_side[half:]))),
            by_row: (add(two[0], got_row[:half]), sides(add_rounded(two[1], got_row[half:]))),
        }

    def finish(parts):
        for i, pair in parts.items():
            reduced[i] = add(*pair) if i == 0 else over(4 * i)(add_rounded(*pair))

    waiting = parts = None
    for pair in pairs:
        first = pair[0]
        if waiting is not None:
            stacks[first], waiting = tie((stacks[first], waiting))
            got = exchange(waiting[1])
        own_out, other_out = expert_rows(*stacks[first], weights)
        if waiting is not None:
            own_out, other_out, got = tie((own_out, other_out, got))
            if parts is not None:
                finish(parts)
            parts = step(*before, waiting[0], got)
        merged = add_rounded(own_out, core(other_out))
        waiting, before = (merged, to_send(merged)), pair
    waiting, cache_lengths = tie((waiting, cache_lengths))
    got = exchange(waiting[1])
    first_context, _ = attend_and_stage(held, cache_lengths, 0, part, ())
    got, parts, first_context, cache_lengths = tie((got, parts, first_context, cache_lengths))
    finish(parts)
    parts = step(*before, waiting[0], got)
    parts, reduced, cache_lengths = tie((parts, reduced, cache_lengths))
    finish(parts)
    second_context, _ = attend_and_stage(
        held, cache_lengths, part, queries.shape[0] - part, ()
    )
    context = jnp.concatenate([first_context, second_context], axis=0)
    total = add_rounded(*(reduced[i] for i in range(planes)))
    partner = sides(total)
    first = lax.axis_index("side") == 0
    moe_out = jnp.concatenate(
        [jnp.where(first, total, partner), jnp.where(first, partner, total)], axis=0
    )
    return (context, moe_out)


def solution(mesh):
    in_specs = (
        P("dev", "side"),
        P("dev", None, "side"),
        P("dev", None, "side"),
        P("dev", "side"),
        P("dev", "side"),
        P("dev"),
        P("dev", None),
        P(),
        P("dev", None),
        P("dev", None),
        P("dev", None, "side"),
        P("dev", None, "side"),
        P("dev", "side", None),
    )
    out_specs = (P("dev", "side"), P("dev", None))
    return jax.shard_map(
        per_device, mesh=mesh, in_specs=in_specs, out_specs=out_specs, check_vma=False
    )
```

```python
import functools

import jax
import jax.numpy as jnp
from jax import lax
from jax.experimental import pallas as pl
from jax.experimental.pallas import tpu as pltpu
from jax.sharding import PartitionSpec as P

HEADS = 64
KV_HEADS = 4
HEAD_DIM = 128


def in_hbm(*arrays):
    return [pltpu.with_memory_space_constraint(a, pltpu.HBM) for a in arrays]


def attend_kernel(
    lengths_ref,
    query_src,
    key_src,
    value_src,
    new_key_src,
    new_value_src,
    *rest,
    start,
    chunk,
    together,
):
    staged = (len(rest) - 9) // 2
    weight_srcs, context_ref, weight_refs = (
        rest[:staged],
        rest[staged],
        rest[staged + 1 : 2 * staged + 1],
    )
    queries, keys, values, new_key, new_value, by_token, mixed, sems = rest[2 * staged + 1 :]
    row_count, cache_len, width = keys.shape
    groups = width // HEAD_DIM
    per_group = HEADS // KV_HEADS
    heads = groups * per_group
    score_scale = HEAD_DIM ** (-0.5)
    small = [
        pltpu.make_async_copy(source.at[pl.ds(start, row_count)], target, sems.at[0, j])
        for j, (source, target) in enumerate(
            ((query_src, queries), (new_key_src, new_key), (new_value_src, new_value))
        )
    ]
    cached = [
        [
            pltpu.make_async_copy(
                source.at[pl.ds(start + low, chunk)],
                target.at[pl.ds(low, chunk)],
                sems.at[1 + j, place],
            )
            for j, (source, target) in enumerate(((key_src, keys), (value_src, values)))
        ]
        for place, low in enumerate(range(0, row_count, chunk))
    ]
    weights = [
        pltpu.make_async_copy(source, target, sems.at[3, j])
        for j, (source, target) in enumerate(zip(weight_srcs, weight_refs))
    ]
    for copy in small + sum(cached, []) + weights:
        copy.start()
    for copy in small:
        copy.wait()
    for head in range(heads):
        columns = slice(head * HEAD_DIM, (head + 1) * HEAD_DIM)
        by_token[pl.ds(head, row_count, stride=heads), :] = queries[:, columns].astype(jnp.float32)
    group_of = lax.broadcasted_iota(jnp.int32, (heads, HEAD_DIM), 0) // per_group
    position = lax.broadcasted_iota(jnp.int32, (heads, cache_len), 1)
    own_keys = new_key[...].astype(jnp.float32)
    own_values = new_value[...].astype(jnp.float32)
    for place, low in enumerate(range(0, row_count, chunk)):
        for copy in cached[place]:
            copy.wait()
        for first in range(low, low + chunk, together):
            tokens = range(first, first + together)
            spread, scores, own_score = [], [], []
            for token in tokens:
                query = by_token[token * heads : (token + 1) * heads, :]
                spread = jnp.concatenate(
                    [jnp.where(group_of == g, query, 0.0) for g in range(groups)], axis=1
                )
                score = lax.dot_general(
                    spread.astype(jnp.bfloat16),
                    keys[token],
                    (((1,), (1,)), ((), ())),
                    preferred_element_type=jnp.float32,
                )
                scores.append(
                    jnp.where(position < lengths_ref[start + token], score * score_scale, -1e30)
                )
                own_score.append(
                    jnp.sum(spread * own_keys[token : token + 1], axis=1, keepdims=True)
                )
            scores = jnp.concatenate(scores, axis=0)
            own_score = jnp.concatenate(own_score, axis=0) * score_scale
            top_score = jnp.maximum(jnp.max(scores, axis=1, keepdims=True), own_score)
            exp_scores = jnp.exp(scores - top_score)
            own_exp = jnp.exp(own_score - top_score)
            inverse = 1.0 / (jnp.sum(exp_scores, axis=1, keepdims=True) + own_exp)
            attn_weights = (exp_scores * inverse).astype(jnp.bfloat16)
            own_prob = (own_exp * inverse).astype(jnp.bfloat16).astype(jnp.float32)
            for place_of, token in enumerate(tokens):
                rows = slice(place_of * heads, (place_of + 1) * heads)
                combined = jnp.dot(
                    attn_weights[rows], values[token], preferred_element_type=jnp.float32
                )
                combined = combined + own_prob[rows] * own_values[token : token + 1]
                picked = combined[:, :HEAD_DIM]
                for g in range(1, groups):
                    columns = slice(g * HEAD_DIM, (g + 1) * HEAD_DIM)
                    picked = jnp.where(group_of == g, combined[:, columns], picked)
                mixed[token * heads : (token + 1) * heads, :] = picked
    for head in range(heads):
        columns = slice(head * HEAD_DIM, (head + 1) * HEAD_DIM)
        context_ref[:, columns] = mixed[pl.ds(head, row_count, stride=heads), :].astype(
            jnp.bfloat16
        )
    for copy in weights:
        copy.wait()


def attend_and_stage(held, cache_lengths, start, row_count, weights):
    width = held[0].shape[1]
    heads = width // HEAD_DIM
    vmem, hbm = pl.BlockSpec(memory_space=pltpu.VMEM), pl.BlockSpec(memory_space=pltpu.HBM)
    chunk = 8
    out = pl.pallas_call(
        functools.partial(attend_kernel, start=start, chunk=chunk, together=8),
        in_specs=[pl.BlockSpec(memory_space=pltpu.SMEM)] + [hbm] * (5 + len(weights)),
        out_specs=[vmem] * (1 + len(weights)),
        out_shape=[jax.ShapeDtypeStruct((row_count, width), held[0].dtype)]
        + [pltpu.VMEM(w.shape, w.dtype) for w in weights],
        scratch_shapes=[pltpu.VMEM((row_count,) + a.shape[1:], a.dtype) for a in held]
        + [pltpu.VMEM(((row_count + 1) * heads, HEAD_DIM), jnp.float32)] * 2
        + [pltpu.SemaphoreType.DMA((4, max(4, -(-row_count // chunk))))],
        compiler_params=pltpu.CompilerParams(vmem_limit_bytes=10 * 1024 * 1024),
        cost_estimate=pl.CostEstimate(
            flops=4 * row_count * heads * held[1].shape[1] * held[1].shape[2],
            bytes_accessed=4 * row_count * held[1].shape[1] * held[1].shape[2]
            + sum(2 * w.size for w in weights),
            transcendentals=row_count * heads * held[1].shape[1],
        ),
        name="attend_and_stage",
    )(cache_lengths, *in_hbm(*held, *weights))
    return out[0], out[1:]


def stage_kernel(*refs):
    count = (len(refs) - 2) // 2
    refs[-2][...] = jnp.zeros(refs[-2].shape, jnp.float32)
    copies = [
        pltpu.make_async_copy(refs[j], refs[count + j], refs[-1].at[j]) for j in range(count)
    ]
    for copy in copies:
        copy.start()
    for copy in copies:
        copy.wait()


def staged(weights):
    return pl.pallas_call(
        stage_kernel,
        in_specs=[pl.BlockSpec(memory_space=pltpu.HBM)] * len(weights),
        out_specs=[pl.BlockSpec(memory_space=pltpu.VMEM)] * (len(weights) + 1),
        out_shape=[pltpu.VMEM(w.shape, w.dtype) for w in weights]
        + [jax.ShapeDtypeStruct((8, 128), jnp.float32)],
        scratch_shapes=[pltpu.SemaphoreType.DMA((len(weights),))],
        compiler_params=pltpu.CompilerParams(vmem_limit_bytes=4 * 1024 * 1024),
        cost_estimate=pl.CostEstimate(
            flops=0, bytes_accessed=sum(4 * w.size for w in weights), transcendentals=0
        ),
        name="stage_weights",
    )(*in_hbm(*weights))


def norm_kernel(side_ref, *refs):
    sources, (rows_ref, half_ref), held, sems = refs[:4], refs[4:6], refs[6:10], refs[10]
    copies = [
        pltpu.make_async_copy(source, target, sems.at[j])
        for j, (source, target) in enumerate(zip(sources, held))
    ]
    for copy in copies:
        copy.start()
    for copy in copies:
        copy.wait()
    hidden_ref, gain_ref, ids_ref, probs_ref = held
    features = hidden_ref.shape[1]
    row_count = hidden_ref.shape[0]
    lanes = rows_ref.shape[1] - features
    wide = hidden_ref[...].astype(jnp.float32)
    inverse = lax.rsqrt(jnp.mean(wide * wide, axis=1, keepdims=True) + 1e-06)
    normed = wide * inverse * gain_ref[...].astype(jnp.float32).reshape(1, features)
    probs = probs_ref[...]
    share = probs / jnp.sum(probs, axis=0, keepdims=True)
    ids = ids_ref[...]
    place = lax.broadcasted_iota(jnp.int32, (lanes, row_count), 0)
    half_lanes = lanes // 2
    expert_of = jnp.where(place < half_lanes, place, place - half_lanes)
    gates = jnp.zeros((lanes, row_count), jnp.float32)
    for k in range(ids.shape[0]):
        gates = gates + jnp.where(expert_of == ids[k : k + 1], share[k : k + 1], 0.0)
    coarse = gates.astype(jnp.bfloat16).astype(jnp.float32)
    gates = jnp.where(place < half_lanes, coarse, gates - coarse).T
    half = row_count // 2
    first = side_ref[0] == 0

    def store(columns, values):
        values = values.astype(jnp.bfloat16)
        mine = jnp.where(first, values[:half], values[half:])
        rows_ref[:half, columns] = mine
        rows_ref[half:, columns] = jnp.where(first, values[half:], values[:half])
        half_ref[:, columns] = mine

    store(slice(0, features), normed)
    store(slice(features, features + lanes), gates)


def normed_rows(hidden, norm_gain, expert_ids, router_probs, experts):
    row_count, features = hidden.shape
    lanes = 128 * (-(-2 * experts // 128))
    side = lax.axis_index("side").astype(jnp.int32).reshape(1)
    width = features + lanes
    vmem, hbm = pl.BlockSpec(memory_space=pltpu.VMEM), pl.BlockSpec(memory_space=pltpu.HBM)
    held = (hidden, norm_gain, expert_ids.T, router_probs.T)
    return pl.pallas_call(
        norm_kernel,
        in_specs=[pl.BlockSpec(memory_space=pltpu.SMEM)] + [hbm] * 4,
        out_specs=(vmem, vmem),
        out_shape=(
            jax.ShapeDtypeStruct((row_count, width), jnp.bfloat16),
            jax.ShapeDtypeStruct((row_count // 2, width), jnp.bfloat16),
        ),
        scratch_shapes=[pltpu.VMEM(a.shape, a.dtype) for a in held]
        + [pltpu.SemaphoreType.DMA((4,))],
        compiler_params=pltpu.CompilerParams(vmem_limit_bytes=8 * 1024 * 1024),
        name="norm_and_gates",
    )(side, *in_hbm(*held))


def expert_kernel(expert_ref, *refs):
    gate_ref, up_ref, down_ref, own_out, other_out, activation = refs[-6:]
    features = gate_ref.shape[1]
    rows = own_out.shape[0]
    x = jnp.concatenate([ref[:, :features] for ref in refs[:-6]], axis=0)
    tail = jnp.concatenate([ref[:, features:] for ref in refs[:-6]], axis=0)
    lanes = tail.shape[1]
    lane = lax.broadcasted_iota(jnp.int32, tail.shape, 1)
    mine = (lane == expert_ref[0]) | (lane == expert_ref[0] + lanes // 2)
    share = jnp.sum(jnp.where(mine, tail.astype(jnp.float32), 0.0), axis=1, keepdims=True)
    for low in range(0, gate_ref.shape[2], 256):
        units = slice(low, low + 256)
        gate_act = jnp.dot(x, gate_ref[0, :, units], preferred_element_type=jnp.float32)
        up_act = jnp.dot(x, up_ref[0, :, units], preferred_element_type=jnp.float32)
        activation[:, units] = (jax.nn.silu(gate_act) * up_act * share).astype(jnp.bfloat16)
    hidden_units = activation[...]
    for low in range(0, features, 1024):
        columns = slice(low, low + 1024)
        part = jnp.dot(
            hidden_units, down_ref[0, :, columns], preferred_element_type=jnp.float32
        ).astype(jnp.bfloat16)
        own_out[:, columns] = part[:rows]
        other_out[:, columns] = part[rows:]


def expert_rows(own, other, weights):
    rows = own.shape[0]
    _, features, hidden_units = weights[0].shape
    expert = lax.axis_index("dev").astype(jnp.int32).reshape(1)
    vmem = pl.BlockSpec(memory_space=pltpu.VMEM)
    return pl.pallas_call(
        expert_kernel,
        in_specs=[pl.BlockSpec(memory_space=pltpu.SMEM)] + [vmem] * 5,
        out_specs=(vmem, vmem),
        out_shape=(jax.ShapeDtypeStruct((rows, features), jnp.bfloat16),) * 2,
        scratch_shapes=[pltpu.VMEM((2 * rows, hidden_units), jnp.bfloat16)],
        compiler_params=pltpu.CompilerParams(vmem_limit_bytes=16 * 1024 * 1024),
        cost_estimate=pl.CostEstimate(
            flops=12 * rows * features * hidden_units,
            bytes_accessed=6 * features * hidden_units,
            transcendentals=2 * rows * hidden_units,
        ),
        name="expert_rows",
    )(
        expert,
        own,
        other,
        *(pltpu.with_memory_space_constraint(w, pltpu.VMEM) for w in weights),
    )


def add(*parts):
    total = parts[0].astype(jnp.float32)
    for part in parts[1:]:
        total = total + part.astype(jnp.float32)
    return total


def add_rounded(*parts):
    return add(*parts).astype(jnp.bfloat16)


def per_device(
    queries,
    cache_keys,
    cache_values,
    new_key,
    new_value,
    cache_lengths,
    hidden,
    norm_gain,
    expert_ids,
    router_probs,
    w_gate,
    w_up,
    w_down,
):
    devices = lax.axis_size("dev")
    planes = devices // 4
    experts = w_gate.shape[0] * devices

    def over(bit):
        return lambda a: lax.ppermute(a, "dev", [(d, d ^ bit) for d in range(devices)])

    core, across = over(1), over(2)
    sides = lambda a: lax.ppermute(a, "side", [(0, 1), (1, 0)])

    def opposite(a):
        pairs = [
            (s * devices + d, (1 - s) * devices + (d ^ 2)) for s in range(2) for d in range(devices)
        ]
        return lax.ppermute(a, ("side", "dev"), pairs)

    own_rows, own_half = normed_rows(hidden, norm_gain, expert_ids, router_probs, experts)
    half = own_half.shape[0]
    tie = lax.optimization_barrier
    held = (queries, cache_keys, cache_values, new_key, new_value)
    part = queries.shape[0] // 2
    direct = [i for i in range(1, planes) if i not in (2, 3)]
    pairs = [(i, i + 2) for i in range(planes) if i % 4 < 2]

    second_half = over(8)(own_half)
    own_of = {i: over(4 * i)(own_rows) for i in direct}
    own_of[0], beside_of = own_rows, {0: across(own_rows)}
    *weights, done = staged((w_gate, w_up, w_down))
    second_half, beside_of[0], done = tie((second_half, beside_of[0], done))
    third_half = over(4)(second_half)

    around = [sides(second_half), across(second_half), opposite(second_half)]
    for i in direct:
        beside_of[i] = over(4 * i)(beside_of[0])
    around = jnp.concatenate(around, axis=0)
    blocks = {i: [own_of[i], beside_of[i]] for i in [0] + direct}
    blocks[2] = [second_half, around]
    blocks[3] = [third_half, over(4)(around)]
    stacks = {}
    for first, second in pairs:
        stack = jnp.concatenate(blocks[first] + blocks[second], axis=0)
        stacks[first] = (stack, core(stack))

    def by_plane(merged):
        rows = [merged[j * half : (j + 1) * half] for j in range(8)]
        return rows[4:], rows[:4]

    def to_send(merged):
        one, two = by_plane(merged)
        return (
            jnp.concatenate([one[1], one[3]], axis=0),
            jnp.concatenate([two[2], two[3]], axis=0),
        )

    reduced = {}

    def exchange(sent):
        return sides(sent[0]), across(sent[1])

    def step(first, second, merged, got):
        one, two = by_plane(merged)
        by_side, by_row = second, first
        got_side, got_row = got
        return {
            by_side: (add(one[0], got_side[:half]), across(add_rounded(one[2], got_side[half:]))),
            by_row: (add(two[0], got_row[:half]), sides(add_rounded(two[1], got_row[half:]))),
        }

    def finish(parts):
        for i, pair in parts.items():
            reduced[i] = add(*pair) if i == 0 else over(4 * i)(add_rounded(*pair))

    waiting = parts = None
    for pair in pairs:
        first = pair[0]
        if waiting is not None:
            stacks[first], waiting = tie((stacks[first], waiting))
            got = exchange(waiting[1])
        own_out, other_out = expert_rows(*stacks[first], weights)
        if waiting is not None:
            own_out, other_out, got = tie((own_out, other_out, got))
            if parts is not None:
                finish(parts)
            parts = step(*before, waiting[0], got)
        merged = add_rounded(own_out, core(other_out))
        waiting, before = (merged, to_send(merged)), pair
    waiting, cache_lengths = tie((waiting, cache_lengths))
    got = exchange(waiting[1])
    first_context, _ = attend_and_stage(held, cache_lengths, 0, part, ())
    got, parts, first_context, cache_lengths = tie((got, parts, first_context, cache_lengths))
    finish(parts)
    parts = step(*before, waiting[0], got)
    parts, reduced, cache_lengths = tie((parts, reduced, cache_lengths))
    finish(parts)
    second_context, _ = attend_and_stage(
        held, cache_lengths, part, queries.shape[0] - part, ()
    )
    context = jnp.concatenate([first_context, second_context], axis=0)
    total = add_rounded(*(reduced[i] for i in range(planes)))
    partner = sides(total)
    low = lax.axis_index("side") * half
    moe_out = jnp.zeros((2 * half, total.shape[1]), total.dtype)
    moe_out = lax.dynamic_update_slice(moe_out, total, (low, 0))
    moe_out = lax.dynamic_update_slice(moe_out, partner, (half - low, 0))
    return (context, moe_out)


def solution(mesh):
    in_specs = (
        P("dev", "side"),
        P("dev", None, "side"),
        P("dev", None, "side"),
        P("dev", "side"),
        P("dev", "side"),
        P("dev"),
        P("dev", None),
        P(),
        P("dev", None),
        P("dev", None),
        P("dev", None, "side"),
        P("dev", None, "side"),
        P("dev", "side", None),
    )
    out_specs = (P("dev", "side"), P("dev", None))
    return jax.shard_map(
        per_device, mesh=mesh, in_specs=in_specs, out_specs=out_specs, check_vma=False
    )
```
